32 devices in a mesh: row: 4 (over z), col: 8 (over y, x, core).
Axes of the slice: x: 2, y: 2, z: 4, core: 2. Of those that a mesh axis runs over, the one named last changes fastest.
Arguments:
- object_field: float32 [2, 1024, 2048], P(None, 'row', 'col'), may hold values from -4 to 4
- probe_field: float32 [2, 256, 256], replicated, may hold values from -6 to 6
- measured: float32 [16, 2048, 256], P('row', 'col'), may hold values from 0.1 to 4
- positions: int32 [16, 16], P('row', 'col'), may hold values from 0 to 160
Outputs:
- new_object: float32 [2, 1024, 2048], P(None, 'row', 'col')
- new_probe: float32 [2, 256, 256], replicated
The draws below stay inside these ranges and needn't reach their ends.
Inputs may be any that keep to these rules, and one draw needn't show every extreme that they name: `positions`: each entry is a pixel offset of a window's top-left corner within its device's tile.
All inputs are finite; a program needn't handle non-finite values.
Results may differ from the reference program's by a relative error of at most 0.0003.
Values sent between devices are 32-bit elements; how exact they have to be, the bound alone decides.
No kernel may reach another device: no remote copies, remote signals or barrier semaphores. Data moves between devices by JAX's collectives and lax.ppermute only.
A program may use at most 64 MiB of HBM per device.

```python
import math
import jax
import jax.numpy as jnp
from jax import lax

F = 256
TILE = 256
FR_DEV = 4
HALO = 160
NY = 1024
NX = 2048
N_ROW = 4
N_COL = 8


def place_ends(result, rng, smallest, top_value):
    dims = result.shape
    index_at = [jax.random.randint(jax.random.fold_in(rng, axis), (), 0, dims[axis]) for axis in range(len(dims))]
    result = result.at[tuple(index_at)].set(smallest)
    longest = dims.index(max(dims))
    index_at[longest] = (index_at[longest] + 1) % dims[longest]
    return result.at[tuple(index_at)].set(top_value)


def shard_levels(rng, shape, cuts, low, high):
    def one(axis_at, shards_of):
        steps = jax.random.uniform(jax.random.fold_in(jax.random.fold_in(rng, 6), axis_at), (shards_of,), jnp.float32, low / len(cuts), high / len(cuts))
        return jnp.repeat(jnp.exp(steps), shape[axis_at] // shards_of).reshape((-1,) + (1,) * (len(shape) - axis_at - 1))

    level = one(*cuts[0])
    for cut in cuts[1:]:
        level = level * one(*cut)
    return level


def normal_values(stream_key, extent, scale, reach, cuts=(), held_as=jnp.bfloat16):
    drawn = jax.random.normal(stream_key, extent, jnp.float32) * scale
    if len(cuts) > 0:
        drawn = shard_levels(stream_key, extent, cuts, -0.22, 0.18) * drawn
    return jnp.clip(drawn, min=-reach, max=reach).astype(held_as)


def setup_inputs(seed: int = 0) -> dict:
    seeds = jax.random.split(jax.random.key(seed), 5)
    return {
        "object_field": normal_values(seeds[0], (2, NY, NX), 0.7, 4.0, ((1, 4), (2, 8)), jnp.float32),
        "probe_field": normal_values(seeds[1], (2, F, F), 1.0, 6.0, (), jnp.float32),
        "measured": jnp.clip(jnp.exp(math.log(4.0) - 3.6888794 * jax.random.uniform(seeds[2], (N_ROW * FR_DEV, N_COL * F, F), jnp.float32) ** shard_levels(seeds[2], (N_ROW * FR_DEV, N_COL * F, F), ((0, 4), (1, 8)), -0.2, 0.2)), 0.1, 4.0),
        "positions": place_ends(jax.random.randint(seeds[3], (N_ROW * FR_DEV, N_COL * 2), 0, HALO + TILE - F + 1), jax.random.fold_in(seeds[3], 1), 0, HALO + TILE - F).astype(jnp.int32),
    }


def reference(object_field, probe_field, measured, positions):
    padded = jnp.pad(object_field, ((0, 0), (0, HALO), (0, HALO)))
    probe_cplx = lax.complex(probe_field[0], probe_field[1])
    per_row = N_COL * FR_DEV

    def one_frame(carry, index):
        grad_acc, probe_acc, inten_acc = carry
        row_dev = index // per_row
        rest = index % per_row
        col_dev = rest // FR_DEV
        frame = rest % FR_DEV
        line = row_dev * FR_DEV + frame
        row_off = positions[line, 2 * col_dev]
        col_off = positions[line, 2 * col_dev + 1]
        top = (row_dev * TILE + row_off).astype(jnp.int32)
        left = (col_dev * TILE + col_off).astype(jnp.int32)
        zero = jnp.int32(0)
        window = lax.dynamic_slice(padded, (zero, top, left), (2, F, F))
        ampl = lax.dynamic_slice(measured, (line.astype(jnp.int32), (col_dev * F).astype(jnp.int32), zero), (1, F, F))[0]
        wind_c = lax.complex(window[0], window[1])
        spectrum = jnp.fft.fft2(probe_cplx * wind_c, norm="ortho")
        factor = ampl / jnp.maximum(jnp.abs(spectrum), 0.5) - 1.0
        change = jnp.fft.ifft2(factor * spectrum, norm="ortho")
        obj_grad = jnp.conj(probe_cplx) * change
        pro_grad = jnp.conj(wind_c) * change
        piece = jnp.stack([jnp.real(obj_grad), jnp.imag(obj_grad)])
        old = lax.dynamic_slice(grad_acc, (zero, top, left), (2, F, F))
        grad_acc = lax.dynamic_update_slice(grad_acc, old + piece, (zero, top, left))
        probe_acc = probe_acc + jnp.stack([jnp.real(pro_grad), jnp.imag(pro_grad)])
        inten_acc = inten_acc + window[0] * window[0] + window[1] * window[1]
        return (grad_acc, probe_acc, inten_acc), None

    init = (jnp.zeros(padded.shape, jnp.float32), jnp.zeros((2, F, F), jnp.float32), jnp.zeros((F, F), jnp.float32))
    count = N_ROW * N_COL * FR_DEV
    (grad_acc, probe_acc, inten_acc), _ = lax.scan(one_frame, init, jnp.arange(count, dtype=jnp.int32))
    grad_obj = grad_acc[:, :NY, :NX]
    largest = jnp.max(probe_field[0] ** 2 + probe_field[1] ** 2)
    new_object = object_field + grad_obj / largest
    new_probe = probe_field + probe_acc / (inten_acc + 1.0)
    return new_object, new_probe
```

```python
import math

import jax
import jax.numpy as jnp
import numpy as np
from jax import lax
from jax.experimental import pallas as pl
from jax.experimental.pallas import tpu as pltpu
from jax.sharding import PartitionSpec as P

HALO = 160
VMEM = pl.BlockSpec(memory_space=pltpu.VMEM)
SMEM = pl.BlockSpec(memory_space=pltpu.SMEM)
LIMIT = 56 * 1024 * 1024


def shifted(value, axis, steps):
    count = lax.axis_size(axis)
    initial, last = (max(0, -steps), min(count, count - steps))
    return lax.ppermute(value, axis, [(source, source + steps) for source in range(initial, last)])


def split_const(matrix):
    high = matrix.astype(jnp.bfloat16)
    low = (matrix - high.astype(np.float64)).astype(jnp.bfloat16)
    return np.stack([high, low])


def tables(side):
    half = side // 2
    index = np.arange(half)
    angle = 2.0 * math.pi / half * (np.outer(index, index) % half)
    cos = np.cos(angle) / math.sqrt(side)
    sin = -np.sin(angle) / math.sqrt(side)
    right = np.block([[cos, sin], [-sin, cos]])
    turn = -2.0 * math.pi / side * index
    tw_cos, tw_sin = (np.cos(turn), np.sin(turn))
    lanes = np.stack([tw_cos, tw_sin]).astype(np.float32)[:, None, :]
    rows = np.stack([tw_cos, tw_sin]).astype(np.float32)[:, :, None] * np.ones((1, 1, half), np.float32)
    pick = np.concatenate([np.arange(0, side, 2), np.arange(1, side, 2)])
    sort = np.zeros((side, side), np.float32)
    sort[pick, np.arange(side)] = 1.0
    return (
        split_const(right),
        split_const(right.T),
        np.broadcast_to(lanes, (2, 8, half)).copy(),
        rows,
        np.stack([sort, sort.T]).astype(jnp.bfloat16),
    )


def dot(left, right):
    return jnp.dot(left, right, preferred_element_type=jnp.float32)


def halves(value):
    high = value.astype(jnp.bfloat16)
    low = (value - high.astype(jnp.float32)).astype(jnp.bfloat16)
    return high, low


def right_mult(value, matrix_ref):
    high, low = halves(value)
    return dot(high, matrix_ref[0]) + (dot(low, matrix_ref[0]) + dot(high, matrix_ref[1]))


def left_mult(matrix_ref, value):
    high, low = halves(value)
    return dot(matrix_ref[0], high) + (dot(matrix_ref[0], low) + dot(matrix_ref[1], high))


def prepare_kernel(pos_ref, probe_ref, meas_ref, sort_ref, prot_ref, sorted_ref):
    frames = meas_ref.shape[0]

    @pl.loop(0, frames)
    def _(frame):
        dy = pos_ref[frame, 0]
        dx = pos_ref[frame, 1]
        for part in range(2):
            prot_ref[frame, part] = pltpu.roll(pltpu.roll(probe_ref[part], dy, 0), dx, 1)
        value = meas_ref[frame]
        total = None
        for _ in range(3):
            piece = value.astype(jnp.bfloat16)
            value = value - piece.astype(jnp.float32)
            term = dot(dot(sort_ref[1], piece).astype(jnp.bfloat16), sort_ref[0])
            total = term if total is None else total + term
        sorted_ref[frame] = total


def frame_kernel(
    pos_ref, tile_ref, right_ref, below_ref, corner_ref, prot_ref, meas_ref, fwd_ref, inv_ref, lane_ref, row_ref,
    gt_ref, gr_ref, gb_ref, gc_ref, qs_ref, max_ref, rpad, bpad, cpad, gra, gba, gca, acc,
):
    frames, side = meas_ref.shape[0], meas_ref.shape[1]
    half = side // 2
    margin = right_ref.shape[2]
    rpad[:, :, 0:margin] = right_ref[...]
    bpad[:, 0:margin, :] = below_ref[...]
    cpad[:, 0:margin, 0:margin] = corner_ref[...]
    gt_ref[...] = jnp.zeros_like(gt_ref)
    gra[...] = jnp.zeros_like(gra)
    gba[...] = jnp.zeros_like(gba)
    gca[...] = jnp.zeros_like(gca)
    acc[...] = jnp.zeros_like(acc)
    rows = lax.broadcasted_iota(jnp.int32, (side, side), 0)
    cols = lax.broadcasted_iota(jnp.int32, (side, side), 1)
    max_ref[0, 0] = jnp.max(prot_ref[0, 0] * prot_ref[0, 0] + prot_ref[0, 1] * prot_ref[0, 1])

    @pl.loop(0, frames)
    def _(frame):
        dy = pos_ref[frame, 0]
        dx = pos_ref[frame, 1]
        own_row = rows >= dy
        own_col = cols >= dx
        obj = [
            jnp.where(
                own_row,
                jnp.where(own_col, tile_ref[part], rpad[part]),
                jnp.where(own_col, bpad[part], cpad[part]),
            )
            for part in range(2)
        ]
        pro_re, pro_im = prot_ref[frame, 0], prot_ref[frame, 1]
        wave_re = pro_re * obj[0] - pro_im * obj[1]
        wave_im = pro_re * obj[1] + pro_im * obj[0]
        lane_cos, lane_sin = lane_ref[0, 0:1], lane_ref[1, 0:1]
        row_cos, row_sin = row_ref[0], row_ref[1]

        even_in = jnp.concatenate([wave_re[:, :half] + wave_re[:, half:], wave_im[:, :half] + wave_im[:, half:]], 1)
        diff_re = wave_re[:, :half] - wave_re[:, half:]
        diff_im = wave_im[:, :half] - wave_im[:, half:]
        odd_in = jnp.concatenate(
            [diff_re * lane_cos - diff_im * lane_sin, diff_re * lane_sin + diff_im * lane_cos], 1
        )
        cols_out = [right_mult(even_in, fwd_ref), right_mult(odd_in, fwd_ref)]

        sums = [value[:half] + value[half:] for value in cols_out]
        diffs = [value[:half] - value[half:] for value in cols_out]
        turned = []
        for value in diffs:
            d_re, d_im = value[:, :half], value[:, half:]
            turned.append((d_re * row_cos - d_im * row_sin, d_re * row_sin + d_im * row_cos))
        even_rows = jnp.concatenate(
            [
                jnp.concatenate([sums[0][:, :half], sums[1][:, :half]], 1),
                jnp.concatenate([sums[0][:, half:], sums[1][:, half:]], 1),
            ],
            0,
        )
        odd_rows = jnp.concatenate(
            [
                jnp.concatenate([turned[0][0], turned[1][0]], 1),
                jnp.concatenate([turned[0][1], turned[1][1]], 1),
            ],
            0,
        )
        back = []
        for which, value in enumerate((even_rows, odd_rows)):
            spec = left_mult(inv_ref, value)
            spec_re, spec_im = spec[:half], spec[half:]
            power = spec_re * spec_re + spec_im * spec_im
            ampl = meas_ref[frame, which * half : (which + 1) * half, :]
            factor = ampl * lax.rsqrt(jnp.maximum(power, 0.25)) - 1.0
            change = jnp.concatenate([factor * spec_re, factor * spec_im], 0)
            back.append(left_mult(fwd_ref, change))
        odd_re, odd_im = back[1][:half], back[1][half:]
        wide_cos = jnp.concatenate([row_cos, row_cos], 1)
        wide_sin = jnp.concatenate([row_sin, row_sin], 1)
        turn_re = odd_re * wide_cos + odd_im * wide_sin
        turn_im = odd_im * wide_cos - odd_re * wide_sin
        mid_re = jnp.concatenate([back[0][:half] + turn_re, back[0][:half] - turn_re], 0)
        mid_im = jnp.concatenate([back[0][half:] + turn_im, back[0][half:] - turn_im], 0)
        even = right_mult(jnp.concatenate([mid_re[:, :half], mid_im[:, :half]], 1), inv_ref)
        odd = right_mult(jnp.concatenate([mid_re[:, half:], mid_im[:, half:]], 1), inv_ref)
        o_re, o_im = odd[:, :half], odd[:, half:]
        turn_re = o_re * lane_cos + o_im * lane_sin
        turn_im = o_im * lane_cos - o_re * lane_sin
        chi_re = jnp.concatenate([even[:, :half] + turn_re, even[:, :half] - turn_re], 1)
        chi_im = jnp.concatenate([even[:, half:] + turn_im, even[:, half:] - turn_im], 1)

        grad = [pro_re * chi_re + pro_im * chi_im, pro_re * chi_im - pro_im * chi_re]
        for part in range(2):
            own = jnp.where(own_row, grad[part], 0.0)
            other = grad[part] - own
            gt_ref[part] += jnp.where(own_col, own, 0.0)
            gra[part] += jnp.where(own_col, 0.0, own)
            gba[part] += jnp.where(own_col, other, 0.0)
            gca[part] += jnp.where(own_col, 0.0, other)
        up = lax.rem(side - dy, side)
        left = lax.rem(side - dx, side)
        for part, value in enumerate(
            (
                obj[0] * chi_re + obj[1] * chi_im,
                obj[0] * chi_im - obj[1] * chi_re,
                obj[0] * obj[0] + obj[1] * obj[1],
            )
        ):
            acc[part] += pltpu.roll(pltpu.roll(value, up, 0), left, 1)

    gr_ref[...] = gra[:, :, 0:margin]
    gb_ref[...] = gba[:, 0:margin, :]
    gc_ref[...] = gca[:, 0:margin, 0:margin]
    blocks, _, depth, _ = qs_ref.shape
    for block in range(blocks):
        qs_ref[block] = acc[:, block * depth : (block + 1) * depth, :]


def f32(*shape):
    return jax.ShapeDtypeStruct(shape, jnp.float32)


def body(object_field, probe_field, measured, positions):
    side = probe_field.shape[1]
    tile = object_field.shape[1]
    margin = HALO
    frames = measured.shape[0]
    n_row, n_col = lax.axis_size("row"), lax.axis_size("col")
    forward, inverse, lane_tw, row_tw, sort = tables(side)
    params = pltpu.CompilerParams(vmem_limit_bytes=LIMIT)

    below = shifted(object_field[:, :margin, :], "row", -1)
    right = shifted(object_field[:, :, :margin], "col", -1)
    corner = shifted(below[:, :, :margin], "col", -1)
    prot, ampl = pl.pallas_call(
        prepare_kernel,
        out_shape=(f32(frames, 2, side, side), f32(frames, side, side)),
        in_specs=[SMEM, VMEM, VMEM, VMEM],
        out_specs=(VMEM, VMEM),
        compiler_params=params,
    )(positions, probe_field, measured, sort)
    depth = side // n_col
    g_tile, g_right, g_below, g_corner, sums, largest = pl.pallas_call(
        frame_kernel,
        out_shape=(
            f32(2, tile, tile),
            f32(2, tile, margin),
            f32(2, margin, tile),
            f32(2, margin, margin),
            f32(n_col, 3, depth, side),
            f32(1, 1),
        ),
        in_specs=[SMEM] + [VMEM] * 10,
        out_specs=(VMEM,) * 5 + (SMEM,),
        scratch_shapes=[pltpu.VMEM((2, side, side), jnp.float32)] * 6 + [pltpu.VMEM((3, side, side), jnp.float32)],
        compiler_params=params,
    )(positions, object_field, right, below, corner, prot, ampl, forward, inverse, lane_tw, row_tw)

    from_corner = shifted(g_corner, "col", 1)
    from_right = shifted(g_right, "col", 1)
    part = jnp.sum(lax.all_to_all(sums, "col", 0, 0), 0)
    from_below = shifted(g_below.at[:, :, :margin].add(from_corner), "row", 1)
    if depth % n_row == 0:
        thin = depth // n_row
        part = part.reshape(3, n_row, thin, side).transpose(1, 0, 2, 3)
        part = jnp.sum(lax.all_to_all(part, "row", 0, 0), 0)
        start = (lax.axis_index("col") * n_row + lax.axis_index("row")) * thin
        old = lax.dynamic_slice_in_dim(probe_field, start, thin, 1)
        new = old + part[:2] / (part[2] + 1.0)
        new = lax.all_to_all(jnp.broadcast_to(new, (n_row,) + new.shape), "row", 0, 0)
    else:
        part = lax.psum(part, "row")
        old = lax.dynamic_slice_in_dim(probe_field, lax.axis_index("col") * depth, depth, 1)
        new = (old + part[:2] / (part[2] + 1.0))[None]
    new = lax.all_to_all(jnp.broadcast_to(new, (n_col,) + new.shape), "col", 0, 0)
    new_probe = new.transpose(2, 0, 1, 3, 4).reshape(2, side, side)
    grad = g_tile.at[:, :, :margin].add(from_right).at[:, :margin, :].add(from_below)
    new_object = object_field + grad / largest[0, 0]
    return (new_object, new_probe)


def solution(mesh):
    in_specs = (P(None, "row", "col"), P(), P("row", "col", None), P("row", "col"))
    out_specs = (P(None, "row", "col"), P())
    return jax.shard_map(body, mesh=mesh, in_specs=in_specs, out_specs=out_specs, check_vma=False)
```

```python
import math

import jax
import jax.numpy as jnp
import numpy as np
from jax import lax
from jax.experimental import pallas as pl
from jax.experimental.pallas import tpu as pltpu
from jax.sharding import PartitionSpec as P

HALO = 160
VMEM = pl.BlockSpec(memory_space=pltpu.VMEM)
SMEM = pl.BlockSpec(memory_space=pltpu.SMEM)
PARAMS = pltpu.CompilerParams(vmem_limit_bytes=24 * 1024 * 1024)
BF16 = jnp.bfloat16


def shifted(value, axis, steps):
    count = lax.axis_size(axis)
    initial, last = (max(0, -steps), min(count, count - steps))
    return lax.ppermute(value, axis, [(source, source + steps) for source in range(initial, last)])


def f32(*shape):
    return jax.ShapeDtypeStruct(shape, jnp.float32)


def cost(flops, moved):
    return pl.CostEstimate(flops=flops, bytes_accessed=moved, transcendentals=0)


def tables(side):
    half = side // 2
    index = np.arange(half)
    angle = 2.0 * math.pi / half * (np.outer(index, index) % half)
    cos = np.cos(angle) / math.sqrt(side)
    sin = -np.sin(angle) / math.sqrt(side)
    matrix = np.block([[cos, sin], [-sin, cos]])
    high = matrix.astype(BF16)
    low = (matrix - high.astype(np.float64)).astype(BF16)
    turn = -2.0 * math.pi / side * index
    twiddle = np.stack([np.cos(turn), np.sin(turn)]).astype(np.float32)
    lanes = np.ascontiguousarray(np.broadcast_to(twiddle[:, None, :], (2, 8, half)))
    rows = np.ascontiguousarray(np.broadcast_to(twiddle[:, :, None], (2, half, half)))
    pick = np.concatenate([np.arange(0, side, 2), np.arange(1, side, 2)])
    sort = np.zeros((side, side), np.float32)
    sort[pick, np.arange(side)] = 1.0
    return (
        np.concatenate([high, high, low], 0),
        np.concatenate([high.T, high.T, low.T], 1),
        np.concatenate([high.T, high.T, low.T], 0),
        np.concatenate([high, high, low], 1),
        lanes,
        rows,
        np.stack([sort, sort.T]).astype(BF16),
    )


def dot(left, right):
    return jnp.dot(left, right, preferred_element_type=jnp.float32)


def halves(value):
    high = value.astype(BF16)
    low = (value - high.astype(jnp.float32)).astype(BF16)
    return high, low


def pack_extra(rows, extra, width):
    per = width // extra
    for group in range(rows // 8):
        yield group * 8, group // per * 8, group % per * extra


def pack_kernel(tile_ref, near_ref, far_ref, right_ref):
    margin = far_ref.shape[1]
    side = tile_ref.shape[1]
    half = far_ref.shape[2]
    extra = margin - half
    near_ref[:, 0:margin, :] = tile_ref[:, 0:margin, 0:half]
    far_ref[...] = tile_ref[:, 0:margin, half:]
    right_ref[:, 0:side, :] = tile_ref[:, :, 0:half]
    for row, packed, lane in pack_extra(side, extra, half):
        piece = tile_ref[:, row : row + 8, half:margin]
        right_ref[:, side + packed : side + packed + 8, lane : lane + extra] = piece
        if row < margin:
            near_ref[:, margin + packed : margin + packed + 8, lane : lane + extra] = piece


def turned(load, steps, half, lanes):
    within = lax.rem(steps, half)
    first = lax.rem(lax.div(steps, half), 2)
    back = lax.rem(half - within, half)
    one = pltpu.roll(load(first), back, 1)
    two = pltpu.roll(load(1 - first), back, 1)
    stay = lanes < half - within
    return jnp.where(stay, one, two), jnp.where(stay, two, one)


def prepare_kernel(pos_ref, probe_ref, meas_ref, sort_ref, prot_ref, sorted_ref, twice):
    frames, side = meas_ref.shape[0], meas_ref.shape[1]
    half = side // 2
    for part in range(2):
        for tile in range(2):
            piece = probe_ref[part, :, tile * half : (tile + 1) * half]
            twice[part, tile, 0:side] = piece
            twice[part, tile, side : 2 * side] = piece
    step = 64
    lanes = lax.broadcasted_iota(jnp.int32, (step, half), 1)

    @pl.loop(0, frames)
    def _(frame):
        dy = pos_ref[0, frame]
        dx = pos_ref[1, frame]
        for part in range(2):
            for row in range(0, side, step):
                one, two = turned(
                    lambda tile: twice[part, tile, pl.ds(side - dy + row, step), :], side - dx, half, lanes
                )
                prot_ref[frame, part, row : row + step, 0:half] = one
                prot_ref[frame, part, row : row + step, half:side] = two
        value = meas_ref[frame]
        total = None
        for _ in range(3):
            piece = value.astype(BF16)
            value = value - piece.astype(jnp.float32)
            term = dot(dot(sort_ref[1], piece).astype(BF16), sort_ref[0])
            total = term if total is None else total + term
        sorted_ref[frame] = total


def frame_kernel(
    pos_ref, tile_ref, right_ref, near_ref, far_ref, corner_ref, prot_ref, meas_ref,
    fwd_right, fwd_left, inv_right, inv_left, lane_ref, row_ref,
    gt_ref, gr_ref, gz_ref, qs_ref, max_ref,
    right_extra, corner_extra, obj_ref, left_in, right_in, mid, twice,
):
    frames, side = meas_ref.shape[0], meas_ref.shape[1]
    half = side // 2
    margin = far_ref.shape[1]
    extra = margin - half
    for row, packed, lane in pack_extra(side, extra, half):
        right_extra[:, row : row + 8, 0:extra] = right_ref[:, side + packed : side + packed + 8, lane : lane + extra]
        if row < margin:
            corner_extra[:, row : row + 8, 0:extra] = corner_ref[
                :, margin + packed : margin + packed + 8, lane : lane + extra
            ]
    lane_cos, lane_sin = lane_ref[0, 0:1], lane_ref[1, 0:1]

    def store_left(where, rows, tile, value):
        high, low = halves(value)
        lane = tile * half
        left_in[where, rows, lane : lane + half] = high
        left_in[where, rows, side + lane : side + lane + half] = low
        left_in[where, rows, 2 * side + lane : 2 * side + lane + half] = high

    def store_right(where, row, count, columns, value):
        high, low = halves(value)
        right_in[where, row : row + count, columns] = high
        right_in[where, side + row : side + row + count, columns] = low
        right_in[where, 2 * side + row : 2 * side + row + count, columns] = high

    step = 32
    lanes = lax.broadcasted_iota(jnp.int32, (step, half), 1)
    row_in = lax.broadcasted_iota(jnp.int32, (step, half), 0)
    largest = jnp.zeros((step, half), jnp.float32)
    for frame in range(frames):
        dy = pos_ref[0, frame]
        dx = pos_ref[1, frame]
        own_col = (lanes >= dx, lanes + half >= dx)
        for row in range(0, side, step):
            rows = slice(row, row + step)
            own_row = row_in + row >= dy
            wave = []
            for tile in range(2):
                columns = slice(tile * half, (tile + 1) * half)
                obj = []
                for part in range(2):
                    right = right_extra[part, rows] if tile else right_ref[part, rows]
                    value = jnp.where(own_col[tile], tile_ref[part, rows, columns], right)
                    if row < margin:
                        below = far_ref[part, rows] if tile else near_ref[part, rows]
                        corner = corner_extra[part, rows] if tile else corner_ref[part, rows]
                        value = jnp.where(own_row, value, jnp.where(own_col[tile], below, corner))
                    obj_ref[frame, part, rows, columns] = value
                    obj.append(value)
                pro_re = prot_ref[frame, 0, rows, columns]
                pro_im = prot_ref[frame, 1, rows, columns]
                if frame == 0:
                    largest = jnp.maximum(largest, pro_re * pro_re + pro_im * pro_im)
                wave.append((pro_re * obj[0] - pro_im * obj[1], pro_re * obj[1] + pro_im * obj[0]))
            (re0, im0), (re1, im1) = wave
            store_left(2 * frame, rows, 0, re0 + re1)
            store_left(2 * frame, rows, 1, im0 + im1)
            re, im = re0 - re1, im0 - im1
            store_left(2 * frame + 1, rows, 0, re * lane_cos - im * lane_sin)
            store_left(2 * frame + 1, rows, 1, re * lane_sin + im * lane_cos)
        for which in range(2):
            mid[2 * frame + which] = dot(left_in[2 * frame + which], fwd_right[...])
    max_ref[0, 0] = jnp.max(largest)

    for frame in range(frames):
        for row in range(0, half, step):
            top, low = slice(row, row + step), slice(half + row, half + row + step)
            row_cos, row_sin = row_ref[0, top], row_ref[1, top]
            for which in range(2):
                columns = slice(which * half, (which + 1) * half)
                top_re, top_im = mid[2 * frame + which, top, 0:half], mid[2 * frame + which, top, half:side]
                low_re, low_im = mid[2 * frame + which, low, 0:half], mid[2 * frame + which, low, half:side]
                store_right(2 * frame, row, step, columns, top_re + low_re)
                store_right(2 * frame, half + row, step, columns, top_im + low_im)
                re, im = top_re - low_re, top_im - low_im
                store_right(2 * frame + 1, row, step, columns, re * row_cos - im * row_sin)
                store_right(2 * frame + 1, half + row, step, columns, re * row_sin + im * row_cos)
        for which in range(2):
            mid[2 * frame + which] = dot(fwd_left[...], right_in[2 * frame + which])

    for frame in range(frames):
        for which in range(2):
            for row in range(0, half, step):
                re = mid[2 * frame + which, row : row + step]
                im = mid[2 * frame + which, half + row : half + row + step]
                ampl = meas_ref[frame, which * half + row : which * half + row + step]
                factor = ampl * lax.rsqrt(jnp.maximum(re * re + im * im, 0.25)) - 1.0
                store_right(2 * frame + which, row, step, slice(0, side), factor * re)
                store_right(2 * frame + which, half + row, step, slice(0, side), factor * im)
            mid[2 * frame + which] = dot(inv_left[...], right_in[2 * frame + which])

    for frame in range(frames):
        for row in range(0, half, step):
            top, low = slice(row, row + step), slice(half + row, half + row + step)
            row_cos, row_sin = row_ref[0, top], row_ref[1, top]
            for which in range(2):
                columns = slice(which * half, (which + 1) * half)
                even_re, even_im = mid[2 * frame, top, columns], mid[2 * frame, low, columns]
                odd_re, odd_im = mid[2 * frame + 1, top, columns], mid[2 * frame + 1, low, columns]
                re = odd_re * row_cos + odd_im * row_sin
                im = odd_im * row_cos - odd_re * row_sin
                store_left(2 * frame + which, top, 0, even_re + re)
                store_left(2 * frame + which, top, 1, even_im + im)
                store_left(2 * frame + which, low, 0, even_re - re)
                store_left(2 * frame + which, low, 1, even_im - im)
        for which in range(2):
            mid[2 * frame + which] = dot(left_in[2 * frame + which], inv_right[...])

    step = 8
    lanes = lax.broadcasted_iota(jnp.int32, (step, half), 1)
    row_in = lax.broadcasted_iota(jnp.int32, (step, half), 0)
    places = {row: (packed, lane) for row, packed, lane in pack_extra(side, extra, half)}
    for row in range(0, side, step):
        rows = slice(row, row + step)
        total = {}
        for frame in range(frames):
            dy = pos_ref[0, frame]
            dx = pos_ref[1, frame]
            own_row = row_in + row >= dy
            even_re, even_im = mid[2 * frame, rows, 0:half], mid[2 * frame, rows, half:side]
            odd_re, odd_im = mid[2 * frame + 1, rows, 0:half], mid[2 * frame + 1, rows, half:side]
            re = odd_re * lane_cos + odd_im * lane_sin
            im = odd_im * lane_cos - odd_re * lane_sin
            for tile in range(2):
                columns = slice(tile * half, (tile + 1) * half)
                chi_re = even_re - re if tile else even_re + re
                chi_im = even_im - im if tile else even_im + im
                own_col = lanes + tile * half >= dx
                pro_re = prot_ref[frame, 0, rows, columns]
                pro_im = prot_ref[frame, 1, rows, columns]
                obj_re = obj_ref[frame, 0, rows, columns]
                obj_im = obj_ref[frame, 1, rows, columns]
                for part, value in enumerate(
                    (pro_re * chi_re + pro_im * chi_im, pro_re * chi_im - pro_im * chi_re)
                ):
                    own = value
                    pieces = []
                    if row < margin:
                        own = jnp.where(own_row, value, 0.0)
                        other = jnp.where(own_row, 0.0, value)
                        pieces.append(("b", jnp.where(own_col, other, 0.0)))
                        pieces.append(("c", jnp.where(own_col, 0.0, other)))
                    pieces.append(("t", jnp.where(own_col, own, 0.0)))
                    pieces.append(("r", jnp.where(own_col, 0.0, own)))
                    for name, piece in pieces:
                        key = (name, part, tile)
                        total[key] = piece if frame == 0 else total[key] + piece
                for index, value in enumerate(
                    (
                        obj_re * chi_re + obj_im * chi_im,
                        obj_re * chi_im - obj_im * chi_re,
                        obj_re * obj_re + obj_im * obj_im,
                    )
                ):
                    twice[frame, index, tile, row : row + step] = value
                    twice[frame, index, tile, side + row : side + row + step] = value
        packed, lane = places[row]
        for part in range(2):
            gt_ref[part, rows, 0:half] = total["t", part, 0]
            gt_ref[part, rows, half:side] = total["t", part, 1]
            gr_ref[part, rows] = total["r", part, 0]
            gr_ref[part, side + packed : side + packed + 8, lane : lane + extra] = total["r", part, 1][:, 0:extra]
            if row < margin:
                gz_ref[part, rows] = total["b", part, 0]
                gz_ref[part, margin + row : margin + row + step] = total["b", part, 1]
                base = 2 * margin
                gz_ref[part, base + row : base + row + step] = total["c", part, 0]
                base = 3 * margin + packed
                gz_ref[part, base : base + 8, lane : lane + extra] = total["c", part, 1][:, 0:extra]

    depth = qs_ref.shape[2]
    step = min(32, depth)
    lanes = lax.broadcasted_iota(jnp.int32, (step, half), 1)
    for row in range(0, side, step):
        for index in range(3):
            sums = None
            for frame in range(frames):
                dy = pos_ref[0, frame]
                dx = pos_ref[1, frame]
                pair = turned(
                    lambda tile: twice[frame, index, tile, pl.ds(dy + row, step), :], dx, half, lanes
                )
                sums = pair if sums is None else (sums[0] + pair[0], sums[1] + pair[1])
            place = slice(row % depth, row % depth + step)
            qs_ref[row // depth, index, place, 0:half] = sums[0]
            qs_ref[row // depth, index, place, half:side] = sums[1]


def finish_kernel(max_ref, tile_ref, grad_ref, right_ref, down_ref, out_ref):
    side = tile_ref.shape[1]
    half = side // 2
    rows = right_ref.shape[1]
    extra = (rows - side) * half // side
    margin = half + extra
    scale = 1.0 / max_ref[0, 0]
    step = 8
    for row, packed, lane in pack_extra(side, extra, half):
        place = slice(row, row + step)
        for part in range(2):
            one = grad_ref[part, place, 0:half] + right_ref[part, place]
            two = grad_ref[part, place, half:side]
            if row < margin:
                one = one + down_ref[part, place]
                two = two + down_ref[part, margin + row : margin + row + step]
            out_ref[part, place, 0:half] = tile_ref[part, place, 0:half] + one * scale
            out_ref[part, place, half:side] = tile_ref[part, place, half:side] + two * scale
            piece = right_ref[part, side + packed : side + packed + 8, lane : lane + extra]
            out_ref[part, place, half:margin] += piece * scale


def body(object_field, probe_field, measured, positions):
    side = probe_field.shape[1]
    half = side // 2
    margin = HALO
    extra = margin - half
    frames = measured.shape[0]
    n_row, n_col = lax.axis_size("row"), lax.axis_size("col")
    fwd_right, fwd_left, inv_right, inv_left, lane_tw, row_tw, sort = tables(side)
    wide = side + side * extra // half
    tall = margin + margin * extra // half

    near, far, right = pl.pallas_call(
        pack_kernel,
        out_shape=(f32(2, tall, half), f32(2, margin, half), f32(2, wide, half)),
        in_specs=[VMEM],
        out_specs=(VMEM,) * 3,
        cost_estimate=cost(10**6, 2 * 10**6),
        compiler_params=PARAMS,
    )(object_field)
    near = shifted(near, "row", -1)
    far = shifted(far, "row", -1)
    right = shifted(right, "col", -1)
    corner = shifted(near, "col", -1)
    places = positions.T
    prot, ampl = pl.pallas_call(
        prepare_kernel,
        out_shape=(f32(frames, 2, side, side), f32(frames, side, side)),
        in_specs=[SMEM, VMEM, VMEM, VMEM],
        out_specs=(VMEM, VMEM),
        scratch_shapes=[pltpu.VMEM((2, 2, 2 * side, half), jnp.float32)],
        cost_estimate=cost(3 * 10**9, 6 * 10**6),
        compiler_params=PARAMS,
    )(places, probe_field, measured, sort)
    depth = side // n_col
    g_tile, g_right, g_down, sums, largest = pl.pallas_call(
        frame_kernel,
        out_shape=(
            f32(2, side, side),
            f32(2, wide, half),
            f32(2, 2 * margin + tall, half),
            f32(n_col, 3, depth, side),
            f32(1, 1),
        ),
        in_specs=[SMEM] + [VMEM] * 13,
        out_specs=(VMEM,) * 4 + (SMEM,),
        scratch_shapes=[
            pltpu.VMEM((2, side, half), jnp.float32),
            pltpu.VMEM((2, margin, half), jnp.float32),
            pltpu.VMEM((frames, 2, side, side), jnp.float32),
            pltpu.VMEM((2 * frames, side, 3 * side), BF16),
            pltpu.VMEM((2 * frames, 3 * side, side), BF16),
            pltpu.VMEM((2 * frames, side, side), jnp.float32),
            pltpu.VMEM((frames, 3, 2, 2 * side, half), jnp.float32),
        ],
        cost_estimate=cost(6 * 10**9, 12 * 10**6),
        compiler_params=PARAMS,
    )(
        places, object_field, right, near, far, corner, prot, ampl,
        fwd_right, fwd_left, inv_right, inv_left, lane_tw, row_tw,
    )

    from_above = shifted(g_down, "row", 1)
    part = jnp.sum(lax.all_to_all(sums, "col", 0, 0), 0)
    g_corner = from_above[:, 2 * margin :]
    g_right, part, g_corner = lax.optimization_barrier((g_right, part, g_corner))
    g_right = jnp.concatenate(
        [
            g_right[:, :margin] + g_corner[:, :margin],
            g_right[:, margin:side],
            g_right[:, side : side + tall - margin] + g_corner[:, margin:],
            g_right[:, side + tall - margin :],
        ],
        1,
    )
    from_left = shifted(g_right, "col", 1)
    if depth % n_row == 0:
        thin = depth // n_row
        part = part.reshape(3, n_row, thin, side).transpose(1, 0, 2, 3)
        part = jnp.sum(lax.all_to_all(part, "row", 0, 0), 0)
        start = (lax.axis_index("col") * n_row + lax.axis_index("row")) * thin
        old = lax.dynamic_slice_in_dim(probe_field, start, thin, 1)
        new = old + part[:2] / (part[2] + 1.0)
        new = lax.all_to_all(jnp.broadcast_to(new, (n_row,) + new.shape), "row", 0, 0)
    else:
        part = lax.psum(part, "row")
        old = lax.dynamic_slice_in_dim(probe_field, lax.axis_index("col") * depth, depth, 1)
        new = (old + part[:2] / (part[2] + 1.0))[None]
    new = lax.all_to_all(jnp.broadcast_to(new, (n_col,) + new.shape), "col", 0, 0)
    new_probe = new.transpose(2, 0, 1, 3, 4).reshape(2, side, side)
    new_object = pl.pallas_call(
        finish_kernel,
        out_shape=f32(2, side, side),
        in_specs=[SMEM] + [VMEM] * 4,
        out_specs=VMEM,
        cost_estimate=cost(10**6, 4 * 10**6),
        compiler_params=PARAMS,
    )(largest, object_field, g_tile, from_left, from_above)
    return (new_object, new_probe)


def solution(mesh):
    in_specs = (P(None, "row", "col"), P(), P("row", "col", None), P("row", "col"))
    out_specs = (P(None, "row", "col"), P())
    return jax.shard_map(body, mesh=mesh, in_specs=in_specs, out_specs=out_specs, check_vma=False)
```

```python
import math

import jax
import jax.numpy as jnp
import numpy as np
from jax import lax
from jax.experimental import pallas as pl
from jax.experimental.pallas import tpu as pltpu
from jax.sharding import PartitionSpec as P

HALO = 160
VMEM = pl.BlockSpec(memory_space=pltpu.VMEM)
HBM = pl.BlockSpec(memory_space=pltpu.HBM)
SMEM = pl.BlockSpec(memory_space=pltpu.SMEM)
PARAMS = pltpu.CompilerParams(vmem_limit_bytes=24 * 1024 * 1024)
BF16 = jnp.bfloat16


def shifted(value, axis, steps):
    count = lax.axis_size(axis)
    initial, last = (max(0, -steps), min(count, count - steps))
    return lax.ppermute(value, axis, [(source, source + steps) for source in range(initial, last)])


def f32(*shape):
    return jax.ShapeDtypeStruct(shape, jnp.float32)


def cost(flops, moved):
    return pl.CostEstimate(flops=flops, bytes_accessed=moved, transcendentals=0)


def tables(side):
    half = side // 2
    index = np.arange(half)
    angle = 2.0 * math.pi / half * (np.outer(index, index) % half)
    cos = np.cos(angle) / math.sqrt(side)
    sin = -np.sin(angle) / math.sqrt(side)
    matrix = np.block([[cos, sin], [-sin, cos]])
    high = matrix.astype(BF16)
    low = (matrix - high.astype(np.float64)).astype(BF16)
    turn = -2.0 * math.pi / side * index
    twiddle = np.stack([np.cos(turn), np.sin(turn)]).astype(np.float32)
    lanes = np.ascontiguousarray(np.broadcast_to(twiddle[:, None, :], (2, 8, half)))
    rows = np.ascontiguousarray(np.broadcast_to(twiddle[:, :, None], (2, half, half)))
    pick = np.concatenate([np.arange(0, side, 2), np.arange(1, side, 2)])
    sort = np.zeros((side, side), np.float32)
    sort[pick, np.arange(side)] = 1.0
    return (
        np.concatenate([high, high, low], 0),
        np.concatenate([high.T, high.T, low.T], 1),
        np.concatenate([high.T, high.T, low.T], 0),
        np.concatenate([high, high, low], 1),
        lanes,
        rows,
        np.stack([sort, sort.T]).astype(BF16),
    )


def dot(left, right):
    return jnp.dot(left, right, preferred_element_type=jnp.float32)


def halves(value):
    high = value.astype(BF16)
    low = (value - high.astype(jnp.float32)).astype(BF16)
    return high, low


def pack_extra(rows, extra, width):
    per = width // extra
    for group in range(rows // 8):
        yield group * 8, group // per * 8, group % per * extra


def pack_kernel(tile_ref, near_ref, far_ref, right_ref):
    margin = far_ref.shape[1]
    side = tile_ref.shape[1]
    half = far_ref.shape[2]
    extra = margin - half
    near_ref[:, 0:margin, :] = tile_ref[:, 0:margin, 0:half]
    far_ref[...] = tile_ref[:, 0:margin, half:]
    right_ref[:, 0:side, :] = tile_ref[:, :, 0:half]
    for row, packed, lane in pack_extra(side, extra, half):
        piece = tile_ref[:, row : row + 8, half:margin]
        right_ref[:, side + packed : side + packed + 8, lane : lane + extra] = piece
        if row < margin:
            near_ref[:, margin + packed : margin + packed + 8, lane : lane + extra] = piece


def turned(load, steps, half, lanes):
    within = lax.rem(steps, half)
    first = lax.rem(lax.div(steps, half), 2)
    back = lax.rem(half - within, half)
    one = pltpu.roll(load(first), back, 1)
    two = pltpu.roll(load(1 - first), back, 1)
    stay = lanes < half - within
    return jnp.where(stay, one, two), jnp.where(stay, two, one)


def prepare_kernel(
    pos_ref, probe_hbm, meas_hbm, sort_hbm, prot_ref, sorted_ref, probe_ref, meas_ref, sort_ref, twice, sems
):
    frames, side = meas_ref.shape[0], meas_ref.shape[1]
    half = side // 2
    pairs = ((probe_hbm, probe_ref), (sort_hbm, sort_ref), (meas_hbm, meas_ref))
    copies = [pltpu.make_async_copy(source, target, sems.at[index]) for index, (source, target) in enumerate(pairs)]
    for copy in copies:
        copy.start()
    copies[0].wait()
    for part in range(2):
        for tile in range(2):
            piece = probe_ref[part, :, tile * half : (tile + 1) * half]
            twice[part, tile, 0:side] = piece
            twice[part, tile, side : 2 * side] = piece
    step = 64
    lanes = lax.broadcasted_iota(jnp.int32, (step, half), 1)

    @pl.loop(0, frames)
    def _(frame):
        dy = pos_ref[0, frame]
        dx = pos_ref[1, frame]
        for part in range(2):
            for row in range(0, side, step):
                one, two = turned(
                    lambda tile: twice[part, tile, pl.ds(side - dy + row, step), :], side - dx, half, lanes
                )
                prot_ref[frame, part, row : row + step, 0:half] = one
                prot_ref[frame, part, row : row + step, half:side] = two

    copies[1].wait()
    copies[2].wait()

    @pl.loop(0, frames)
    def _(frame):
        value = meas_ref[frame]
        total = None
        for _ in range(3):
            piece = value.astype(BF16)
            value = value - piece.astype(jnp.float32)
            term = dot(dot(sort_ref[1], piece).astype(BF16), sort_ref[0])
            total = term if total is None else total + term
        sorted_ref[frame] = total


def frame_kernel(
    pos_ref, tile_ref, right_ref, near_ref, far_ref, corner_ref, prot_ref, meas_ref,
    fwd_right, fwd_left, inv_right, inv_left, lane_ref, row_ref,
    gt_ref, gr_ref, gz_ref, qs_ref, max_ref,
    right_extra, corner_extra, obj_ref, left_in, right_in, mid, twice,
):
    frames, side = meas_ref.shape[0], meas_ref.shape[1]
    half = side // 2
    margin = far_ref.shape[1]
    wide = right_ref.shape[1]
    extra = margin - half
    for row, packed, lane in pack_extra(side, extra, half):
        right_extra[:, row : row + 8, 0:extra] = right_ref[:, side + packed : side + packed + 8, lane : lane + extra]
        if row < margin:
            corner_extra[:, row : row + 8, 0:extra] = corner_ref[
                :, margin + packed : margin + packed + 8, lane : lane + extra
            ]
    lane_cos, lane_sin = lane_ref[0, 0:1], lane_ref[1, 0:1]

    def store_left(where, rows, tile, value):
        high, low = halves(value)
        lane = tile * half
        left_in[where, rows, lane : lane + half] = high
        left_in[where, rows, side + lane : side + lane + half] = low
        left_in[where, rows, 2 * side + lane : 2 * side + lane + half] = high

    def store_right(where, row, count, columns, value):
        high, low = halves(value)
        right_in[where, row : row + count, columns] = high
        right_in[where, side + row : side + row + count, columns] = low
        right_in[where, 2 * side + row : 2 * side + row + count, columns] = high

    step = 32
    lanes = lax.broadcasted_iota(jnp.int32, (step, half), 1)
    row_in = lax.broadcasted_iota(jnp.int32, (step, half), 0)
    largest = jnp.zeros((step, half), jnp.float32)
    for frame in range(frames):
        dy = pos_ref[0, frame]
        dx = pos_ref[1, frame]
        own_col = (lanes >= dx, lanes + half >= dx)
        for row in range(0, side, step):
            rows = slice(row, row + step)
            own_row = row_in + row >= dy
            wave = []
            for tile in range(2):
                columns = slice(tile * half, (tile + 1) * half)
                obj = []
                for part in range(2):
                    right = right_extra[part, rows] if tile else right_ref[part, rows]
                    value = jnp.where(own_col[tile], tile_ref[part, rows, columns], right)
                    if row < margin:
                        below = far_ref[part, rows] if tile else near_ref[part, rows]
                        corner = corner_extra[part, rows] if tile else corner_ref[part, rows]
                        value = jnp.where(own_row, value, jnp.where(own_col[tile], below, corner))
                    obj_ref[frame, part, rows, columns] = value
                    obj.append(value)
                pro_re = prot_ref[frame, 0, rows, columns]
                pro_im = prot_ref[frame, 1, rows, columns]
                if frame == 0:
                    largest = jnp.maximum(largest, pro_re * pro_re + pro_im * pro_im)
                wave.append((pro_re * obj[0] - pro_im * obj[1], pro_re * obj[1] + pro_im * obj[0]))
            (re0, im0), (re1, im1) = wave
            store_left(2 * frame, rows, 0, re0 + re1)
            store_left(2 * frame, rows, 1, im0 + im1)
            re, im = re0 - re1, im0 - im1
            store_left(2 * frame + 1, rows, 0, re * lane_cos - im * lane_sin)
            store_left(2 * frame + 1, rows, 1, re * lane_sin + im * lane_cos)
        for which in range(2):
            mid[2 * frame + which] = dot(left_in[2 * frame + which], fwd_right[...])
    max_ref[0, 0] = jnp.max(largest)

    for frame in range(frames):
        for row in range(0, half, step):
            top, low = slice(row, row + step), slice(half + row, half + row + step)
            row_cos, row_sin = row_ref[0, top], row_ref[1, top]
            for which in range(2):
                columns = slice(which * half, (which + 1) * half)
                top_re, top_im = mid[2 * frame + which, top, 0:half], mid[2 * frame + which, top, half:side]
                low_re, low_im = mid[2 * frame + which, low, 0:half], mid[2 * frame + which, low, half:side]
                store_right(2 * frame, row, step, columns, top_re + low_re)
                store_right(2 * frame, half + row, step, columns, top_im + low_im)
                re, im = top_re - low_re, top_im - low_im
                store_right(2 * frame + 1, row, step, columns, re * row_cos - im * row_sin)
                store_right(2 * frame + 1, half + row, step, columns, re * row_sin + im * row_cos)
        for which in range(2):
            mid[2 * frame + which] = dot(fwd_left[...], right_in[2 * frame + which])

    for frame in range(frames):
        for which in range(2):
            for row in range(0, half, step):
                re = mid[2 * frame + which, row : row + step]
                im = mid[2 * frame + which, half + row : half + row + step]
                ampl = meas_ref[frame, which * half + row : which * half + row + step]
                factor = ampl * lax.rsqrt(jnp.maximum(re * re + im * im, 0.25)) - 1.0
                store_right(2 * frame + which, row, step, slice(0, side), factor * re)
                store_right(2 * frame + which, half + row, step, slice(0, side), factor * im)
            mid[2 * frame + which] = dot(inv_left[...], right_in[2 * frame + which])

    for frame in range(frames):
        for row in range(0, half, step):
            top, low = slice(row, row + step), slice(half + row, half + row + step)
            row_cos, row_sin = row_ref[0, top], row_ref[1, top]
            for which in range(2):
                columns = slice(which * half, (which + 1) * half)
                even_re, even_im = mid[2 * frame, top, columns], mid[2 * frame, low, columns]
                odd_re, odd_im = mid[2 * frame + 1, top, columns], mid[2 * frame + 1, low, columns]
                re = odd_re * row_cos + odd_im * row_sin
                im = odd_im * row_cos - odd_re * row_sin
                store_left(2 * frame + which, top, 0, even_re + re)
                store_left(2 * frame + which, top, 1, even_im + im)
                store_left(2 * frame + which, low, 0, even_re - re)
                store_left(2 * frame + which, low, 1, even_im - im)
        for which in range(2):
            mid[2 * frame + which] = dot(left_in[2 * frame + which], inv_right[...])

    step = 8
    lanes = lax.broadcasted_iota(jnp.int32, (step, half), 1)
    row_in = lax.broadcasted_iota(jnp.int32, (step, half), 0)
    places = {row: (packed, lane) for row, packed, lane in pack_extra(side, extra, half)}
    for row in range(0, side, step):
        rows = slice(row, row + step)
        total = {}
        for frame in range(frames):
            dy = pos_ref[0, frame]
            dx = pos_ref[1, frame]
            own_row = row_in + row >= dy
            even_re, even_im = mid[2 * frame, rows, 0:half], mid[2 * frame, rows, half:side]
            odd_re, odd_im = mid[2 * frame + 1, rows, 0:half], mid[2 * frame + 1, rows, half:side]
            re = odd_re * lane_cos + odd_im * lane_sin
            im = odd_im * lane_cos - odd_re * lane_sin
            for tile in range(2):
                columns = slice(tile * half, (tile + 1) * half)
                chi_re = even_re - re if tile else even_re + re
                chi_im = even_im - im if tile else even_im + im
                own_col = lanes + tile * half >= dx
                pro_re = prot_ref[frame, 0, rows, columns]
                pro_im = prot_ref[frame, 1, rows, columns]
                obj_re = obj_ref[frame, 0, rows, columns]
                obj_im = obj_ref[frame, 1, rows, columns]
                for part, value in enumerate(
                    (pro_re * chi_re + pro_im * chi_im, pro_re * chi_im - pro_im * chi_re)
                ):
                    own = value
                    pieces = []
                    if row < margin:
                        own = jnp.where(own_row, value, 0.0)
                        other = jnp.where(own_row, 0.0, value)
                        pieces.append(("b", jnp.where(own_col, other, 0.0)))
                        pieces.append(("c", jnp.where(own_col, 0.0, other)))
                    pieces.append(("t", jnp.where(own_col, own, 0.0)))
                    pieces.append(("r", jnp.where(own_col, 0.0, own)))
                    for name, piece in pieces:
                        key = (name, part, tile)
                        total[key] = piece if frame == 0 else total[key] + piece
                for index, value in enumerate(
                    (
                        obj_re * chi_re + obj_im * chi_im,
                        obj_re * chi_im - obj_im * chi_re,
                        obj_re * obj_re + obj_im * obj_im,
                    )
                ):
                    twice[frame, index, tile, row : row + step] = value
                    twice[frame, index, tile, side + row : side + row + step] = value
        packed, lane = places[row]
        for part in range(2):
            gt_ref[part, rows, 0:half] = total["t", part, 0]
            gt_ref[part, rows, half:side] = total["t", part, 1]
            gr_ref[part, rows] = total["r", part, 0]
            gr_ref[part, side + packed : side + packed + 8, lane : lane + extra] = total["r", part, 1][:, 0:extra]
            if row < margin:
                gz_ref[part, rows] = total["b", part, 0]
                gz_ref[part, margin + row : margin + row + step] = total["b", part, 1]
                gr_ref[part, wide + row : wide + row + step] = total["c", part, 0]
                base = wide + margin + packed
                gr_ref[part, base : base + 8, lane : lane + extra] = total["c", part, 1][:, 0:extra]

    depth = qs_ref.shape[2]
    step = min(32, depth)
    lanes = lax.broadcasted_iota(jnp.int32, (step, half), 1)
    for row in range(0, side, step):
        for index in range(3):
            sums = None
            for frame in range(frames):
                dy = pos_ref[0, frame]
                dx = pos_ref[1, frame]
                pair = turned(
                    lambda tile: twice[frame, index, tile, pl.ds(dy + row, step), :], dx, half, lanes
                )
                sums = pair if sums is None else (sums[0] + pair[0], sums[1] + pair[1])
            place = slice(row % depth, row % depth + step)
            qs_ref[row // depth, index, place, 0:half] = sums[0]
            qs_ref[row // depth, index, place, half:side] = sums[1]


def finish_kernel(max_ref, tile_ref, grad_ref, right_ref, down_ref, corner_ref, out_ref):
    side = tile_ref.shape[1]
    half = side // 2
    margin = down_ref.shape[1] // 2
    extra = margin - half
    scale = 1.0 / max_ref[0, 0]
    step = 8
    for row, packed, lane in pack_extra(side, extra, half):
        place = slice(row, row + step)
        for part in range(2):
            one = grad_ref[part, place, 0:half] + right_ref[part, place]
            two = grad_ref[part, place, half:side]
            piece = right_ref[part, side + packed : side + packed + 8, lane : lane + extra]
            if row < margin:
                one = one + down_ref[part, place] + corner_ref[part, place]
                two = two + down_ref[part, margin + row : margin + row + step]
                piece = piece + corner_ref[part, margin + packed : margin + packed + 8, lane : lane + extra]
            out_ref[part, place, 0:half] = tile_ref[part, place, 0:half] + one * scale
            out_ref[part, place, half:side] = tile_ref[part, place, half:side] + two * scale
            out_ref[part, place, half:margin] += piece * scale


def body(object_field, probe_field, measured, positions):
    side = probe_field.shape[1]
    half = side // 2
    margin = HALO
    extra = margin - half
    frames = measured.shape[0]
    n_row, n_col = lax.axis_size("row"), lax.axis_size("col")
    fwd_right, fwd_left, inv_right, inv_left, lane_tw, row_tw, sort = tables(side)
    wide = side + side * extra // half
    tall = margin + margin * extra // half

    near, far, right = pl.pallas_call(
        pack_kernel,
        out_shape=(f32(2, tall, half), f32(2, margin, half), f32(2, wide, half)),
        in_specs=[VMEM],
        out_specs=(VMEM,) * 3,
        cost_estimate=cost(10**6, 2 * 10**6),
        compiler_params=PARAMS,
    )(object_field)
    near = shifted(near, "row", -1)
    far = shifted(far, "row", -1)
    right = shifted(right, "col", -1)
    places = positions.T
    prot, ampl = pl.pallas_call(
        prepare_kernel,
        out_shape=(f32(frames, 2, side, side), f32(frames, side, side)),
        in_specs=[SMEM, HBM, HBM, HBM],
        out_specs=(VMEM, VMEM),
        scratch_shapes=[
            pltpu.VMEM((2, side, side), jnp.float32),
            pltpu.VMEM((frames, side, side), jnp.float32),
            pltpu.VMEM((2, side, side), BF16),
            pltpu.VMEM((2, 2, 2 * side, half), jnp.float32),
            pltpu.SemaphoreType.DMA((3,)),
        ],
        cost_estimate=cost(3 * 10**9, 6 * 10**6),
        compiler_params=pltpu.CompilerParams(vmem_limit_bytes=60 * 1024 * 1024),
    )(places, probe_field, measured, sort)
    near, prot = lax.optimization_barrier((near, prot))
    corner = shifted(near, "col", -1)
    depth = side // n_col
    g_tile, g_right, g_down, sums, largest = pl.pallas_call(
        frame_kernel,
        out_shape=(
            f32(2, side, side),
            f32(2, wide + tall, half),
            f32(2, 2 * margin, half),
            f32(n_col, 3, depth, side),
            f32(1, 1),
        ),
        in_specs=[SMEM] + [VMEM] * 13,
        out_specs=(VMEM,) * 4 + (SMEM,),
        scratch_shapes=[
            pltpu.VMEM((2, side, half), jnp.float32),
            pltpu.VMEM((2, margin, half), jnp.float32),
            pltpu.VMEM((frames, 2, side, side), jnp.float32),
            pltpu.VMEM((2 * frames, side, 3 * side), BF16),
            pltpu.VMEM((2 * frames, 3 * side, side), BF16),
            pltpu.VMEM((2 * frames, side, side), jnp.float32),
            pltpu.VMEM((frames, 3, 2, 2 * side, half), jnp.float32),
        ],
        cost_estimate=cost(6 * 10**9, 12 * 10**6),
        compiler_params=PARAMS,
    )(
        places, object_field, right, near, far, corner, prot, ampl,
        fwd_right, fwd_left, inv_right, inv_left, lane_tw, row_tw,
    )

    from_above = shifted(g_down, "row", 1)
    part = jnp.sum(lax.all_to_all(sums, "col", 0, 0), 0)
    g_right, part = lax.optimization_barrier((g_right, part))
    from_left = shifted(g_right, "col", 1)
    first, second = part[:, : depth // 2], part[:, depth // 2 :]
    first = lax.psum(first, "row")
    first, second = lax.optimization_barrier((first, second))
    second = lax.psum(second, "row")
    part = jnp.concatenate([first, second], 1)
    old = lax.dynamic_slice_in_dim(probe_field, lax.axis_index("col") * depth, depth, 1)
    new = old + part[:2] / (part[2] + 1.0)
    new, from_left = lax.optimization_barrier((new, from_left))
    new = lax.all_to_all(jnp.broadcast_to(new, (n_col,) + new.shape), "col", 0, 0)
    from_corner = shifted(from_left[:, wide:], "row", 1)
    new_probe = new.transpose(1, 0, 2, 3).reshape(2, side, side)
    new_object = pl.pallas_call(
        finish_kernel,
        out_shape=f32(2, side, side),
        in_specs=[SMEM] + [VMEM] * 5,
        out_specs=VMEM,
        cost_estimate=cost(10**6, 4 * 10**6),
        compiler_params=PARAMS,
    )(largest, object_field, g_tile, from_left, from_above, from_corner)
    return (new_object, new_probe)


def solution(mesh):
    in_specs = (P(None, "row", "col"), P(), P("row", "col", None), P("row", "col"))
    out_specs = (P(None, "row", "col"), P())
    return jax.shard_map(body, mesh=mesh, in_specs=in_specs, out_specs=out_specs, check_vma=False)
```

```python
import math

import jax
import jax.numpy as jnp
import numpy as np
from jax import lax
from jax.experimental import pallas as pl
from jax.experimental.pallas import tpu as pltpu
from jax.sharding import PartitionSpec as P

HALO = 160
VMEM = pl.BlockSpec(memory_space=pltpu.VMEM)
SMEM = pl.BlockSpec(memory_space=pltpu.SMEM)
PARAMS = pltpu.CompilerParams(vmem_limit_bytes=24 * 1024 * 1024)
BF16 = jnp.bfloat16


def shifted(value, axis, steps):
    count = lax.axis_size(axis)
    initial, last = (max(0, -steps), min(count, count - steps))
    return lax.ppermute(value, axis, [(source, source + steps) for source in range(initial, last)])


def diagonal(value):
    rows, cols = lax.axis_size("row"), lax.axis_size("col")
    pairs = [
        ((row + 1) * cols + col + 1, row * cols + col) for row in range(rows - 1) for col in range(cols - 1)
    ]
    return lax.ppermute(value, ("row", "col"), pairs)


def row_sum(value):
    rows = lax.axis_size("row")
    if rows != 4:
        return lax.psum(value, "row")
    one, two, three = (
        lax.ppermute(value, "row", [(row, row ^ step) for row in range(rows)]) for step in (1, 2, 3)
    )
    return (value + one) + (two + three)


def f32(*shape):
    return jax.ShapeDtypeStruct(shape, jnp.float32)


def cost(flops, moved):
    return pl.CostEstimate(flops=flops, bytes_accessed=moved, transcendentals=0)


def tables(side):
    half = side // 2
    index = np.arange(half)
    angle = 2.0 * math.pi / half * (np.outer(index, index) % half)
    cos = np.cos(angle) / math.sqrt(side)
    sin = -np.sin(angle) / math.sqrt(side)
    matrix = np.block([[cos, sin], [-sin, cos]])
    high = matrix.astype(BF16)
    low = (matrix - high.astype(np.float64)).astype(BF16)
    turn = -2.0 * math.pi / side * index
    twiddle = np.stack([np.cos(turn), np.sin(turn)]).astype(np.float32)
    lanes = np.ascontiguousarray(np.broadcast_to(twiddle[:, None, :], (2, 8, half)))
    rows = np.ascontiguousarray(np.broadcast_to(twiddle[:, :, None], (2, half, half)))
    return (
        np.concatenate([high, high, low], 0),
        np.concatenate([high.T, high.T, low.T], 1),
        np.concatenate([high.T, high.T, low.T], 0),
        np.concatenate([high, high, low], 1),
        lanes,
        rows,
    )


def dot(left, right):
    return jnp.dot(left, right, preferred_element_type=jnp.float32)


def halves(value):
    high = value.astype(BF16)
    low = (value - high.astype(jnp.float32)).astype(BF16)
    return high, low


def pack_extra(rows, extra, width):
    per = width // extra
    for group in range(rows // 8):
        yield group * 8, group // per * 8, group % per * extra


def pack_kernel(tile_ref, below_ref, corner_ref, right_ref):
    side = tile_ref.shape[1]
    half = side // 2
    margin = below_ref.shape[1] // 2
    extra = margin - half
    below_ref[:, 0:margin, :] = tile_ref[:, 0:margin, 0:half]
    below_ref[:, margin : 2 * margin, :] = tile_ref[:, 0:margin, half:]
    corner_ref[:, 0:margin, :] = tile_ref[:, 0:margin, 0:half]
    right_ref[:, 0:side, :] = tile_ref[:, :, 0:half]
    for row, packed, lane in pack_extra(side, extra, half):
        piece = tile_ref[:, row : row + 8, half:margin]
        right_ref[:, side + packed : side + packed + 8, lane : lane + extra] = piece
        if row < margin:
            corner_ref[:, margin + packed : margin + packed + 8, lane : lane + extra] = piece


def turned(load, steps, half, lanes):
    within = lax.rem(steps, half)
    first = lax.rem(lax.div(steps, half), 2)
    back = lax.rem(half - within, half)
    one = pltpu.roll(load(first), back, 1)
    two = pltpu.roll(load(1 - first), back, 1)
    stay = lanes < half - within
    return jnp.where(stay, one, two), jnp.where(stay, two, one)


def prepare_kernel(pos_ref, probe_ref, meas_ref, prot_ref, sorted_ref, twice):
    frames, side = meas_ref.shape[0], meas_ref.shape[1]
    half = side // 2
    for part in range(2):
        for tile in range(2):
            piece = probe_ref[part, :, tile * half : (tile + 1) * half]
            twice[part, tile, 0:side] = piece
            twice[part, tile, side : 2 * side] = piece
    step = 64
    lanes = lax.broadcasted_iota(jnp.int32, (step, half), 1)
    rows = lax.broadcasted_iota(jnp.int32, (side, side), 0)
    cols = lax.broadcasted_iota(jnp.int32, (side, side), 1)
    sort = jnp.where(rows == jnp.where(cols < half, 2 * cols, 2 * cols - side + 1), 1.0, 0.0).astype(BF16)
    unsort = jnp.where(cols == jnp.where(rows < half, 2 * rows, 2 * rows - side + 1), 1.0, 0.0).astype(BF16)

    @pl.loop(0, frames)
    def _(frame):
        dy = pos_ref[0, frame]
        dx = pos_ref[1, frame]
        for part in range(2):
            for row in range(0, side, step):
                one, two = turned(
                    lambda tile: twice[part, tile, pl.ds(side - dy + row, step), :], side - dx, half, lanes
                )
                prot_ref[frame, part, row : row + step, 0:half] = one
                prot_ref[frame, part, row : row + step, half:side] = two
        value = meas_ref[frame]
        total = None
        for _ in range(3):
            piece = value.astype(BF16)
            value = value - piece.astype(jnp.float32)
            term = dot(dot(unsort, piece).astype(BF16), sort)
            total = term if total is None else total + term
        sorted_ref[frame] = total


def frame_kernel(
    pos_ref, tile_ref, right_ref, below_ref, corner_ref, prot_ref, meas_ref,
    fwd_right, fwd_left, inv_right, inv_left, lane_ref, row_ref,
    gt_ref, gr_ref, gz_ref, qs_ref, max_ref,
    right_extra, corner_extra, obj_ref, left_in, right_in, mid, twice,
):
    frames, side = meas_ref.shape[0], meas_ref.shape[1]
    half = side // 2
    margin = below_ref.shape[1] // 2
    wide = right_ref.shape[1]
    extra = margin - half
    for row, packed, lane in pack_extra(side, extra, half):
        right_extra[:, row : row + 8, 0:extra] = right_ref[:, side + packed : side + packed + 8, lane : lane + extra]
        if row < margin:
            corner_extra[:, row : row + 8, 0:extra] = corner_ref[
                :, margin + packed : margin + packed + 8, lane : lane + extra
            ]
    lane_cos, lane_sin = lane_ref[0, 0:1], lane_ref[1, 0:1]

    def store_left(where, rows, tile, value):
        high, low = halves(value)
        lane = tile * half
        left_in[where, rows, lane : lane + half] = high
        left_in[where, rows, side + lane : side + lane + half] = low
        left_in[where, rows, 2 * side + lane : 2 * side + lane + half] = high

    def store_right(where, row, count, columns, value):
        high, low = halves(value)
        right_in[where, row : row + count, columns] = high
        right_in[where, side + row : side + row + count, columns] = low
        right_in[where, 2 * side + row : 2 * side + row + count, columns] = high

    step = 32
    lanes = lax.broadcasted_iota(jnp.int32, (step, half), 1)
    row_in = lax.broadcasted_iota(jnp.int32, (step, half), 0)
    largest = jnp.zeros((step, half), jnp.float32)
    for frame in range(frames):
        dy = pos_ref[0, frame]
        dx = pos_ref[1, frame]
        own_col = (lanes >= dx, lanes + half >= dx)
        for row in range(0, side, step):
            rows = slice(row, row + step)
            own_row = row_in + row >= dy
            wave = []
            for tile in range(2):
                columns = slice(tile * half, (tile + 1) * half)
                obj = []
                for part in range(2):
                    right = right_extra[part, rows] if tile else right_ref[part, rows]
                    value = jnp.where(own_col[tile], tile_ref[part, rows, columns], right)
                    if row < margin:
                        below = below_ref[part, tile * margin + row : tile * margin + row + step]
                        corner = corner_extra[part, rows] if tile else corner_ref[part, rows]
                        value = jnp.where(own_row, value, jnp.where(own_col[tile], below, corner))
                    obj_ref[frame, part, rows, columns] = value
                    obj.append(value)
                pro_re = prot_ref[frame, 0, rows, columns]
                pro_im = prot_ref[frame, 1, rows, columns]
                if frame == 0:
                    largest = jnp.maximum(largest, pro_re * pro_re + pro_im * pro_im)
                wave.append((pro_re * obj[0] - pro_im * obj[1], pro_re * obj[1] + pro_im * obj[0]))
            (re0, im0), (re1, im1) = wave
            store_left(2 * frame, rows, 0, re0 + re1)
            store_left(2 * frame, rows, 1, im0 + im1)
            re, im = re0 - re1, im0 - im1
            store_left(2 * frame + 1, rows, 0, re * lane_cos - im * lane_sin)
            store_left(2 * frame + 1, rows, 1, re * lane_sin + im * lane_cos)
        for which in range(2):
            mid[2 * frame + which] = dot(left_in[2 * frame + which], fwd_right[...])
    max_ref[0, 0] = jnp.max(largest)

    for frame in range(frames):
        for row in range(0, half, step):
            top, low = slice(row, row + step), slice(half + row, half + row + step)
            row_cos, row_sin = row_ref[0, top], row_ref[1, top]
            for which in range(2):
                columns = slice(which * half, (which + 1) * half)
                top_re, top_im = mid[2 * frame + which, top, 0:half], mid[2 * frame + which, top, half:side]
                low_re, low_im = mid[2 * frame + which, low, 0:half], mid[2 * frame + which, low, half:side]
                store_right(2 * frame, row, step, columns, top_re + low_re)
                store_right(2 * frame, half + row, step, columns, top_im + low_im)
                re, im = top_re - low_re, top_im - low_im
                store_right(2 * frame + 1, row, step, columns, re * row_cos - im * row_sin)
                store_right(2 * frame + 1, half + row, step, columns, re * row_sin + im * row_cos)
        for which in range(2):
            mid[2 * frame + which] = dot(fwd_left[...], right_in[2 * frame + which])

    for frame in range(frames):
        for which in range(2):
            for row in range(0, half, step):
                re = mid[2 * frame + which, row : row + step]
                im = mid[2 * frame + which, half + row : half + row + step]
                ampl = meas_ref[frame, which * half + row : which * half + row + step]
                factor = ampl * lax.rsqrt(jnp.maximum(re * re + im * im, 0.25)) - 1.0
                store_right(2 * frame + which, row, step, slice(0, side), factor * re)
                store_right(2 * frame + which, half + row, step, slice(0, side), factor * im)
            mid[2 * frame + which] = dot(inv_left[...], right_in[2 * frame + which])

    for frame in range(frames):
        for row in range(0, half, step):
            top, low = slice(row, row + step), slice(half + row, half + row + step)
            row_cos, row_sin = row_ref[0, top], row_ref[1, top]
            for which in range(2):
                columns = slice(which * half, (which + 1) * half)
                even_re, even_im = mid[2 * frame, top, columns], mid[2 * frame, low, columns]
                odd_re, odd_im = mid[2 * frame + 1, top, columns], mid[2 * frame + 1, low, columns]
                re = odd_re * row_cos + odd_im * row_sin
                im = odd_im * row_cos - odd_re * row_sin
                store_left(2 * frame + which, top, 0, even_re + re)
                store_left(2 * frame + which, top, 1, even_im + im)
                store_left(2 * frame + which, low, 0, even_re - re)
                store_left(2 * frame + which, low, 1, even_im - im)
        for which in range(2):
            mid[2 * frame + which] = dot(left_in[2 * frame + which], inv_right[...])

    step = 8
    lanes = lax.broadcasted_iota(jnp.int32, (step, half), 1)
    row_in = lax.broadcasted_iota(jnp.int32, (step, half), 0)
    places = {row: (packed, lane) for row, packed, lane in pack_extra(side, extra, half)}
    for row in range(0, side, step):
        rows = slice(row, row + step)
        total = {}
        for frame in range(frames):
            dy = pos_ref[0, frame]
            dx = pos_ref[1, frame]
            own_row = row_in + row >= dy
            even_re, even_im = mid[2 * frame, rows, 0:half], mid[2 * frame, rows, half:side]
            odd_re, odd_im = mid[2 * frame + 1, rows, 0:half], mid[2 * frame + 1, rows, half:side]
            re = odd_re * lane_cos + odd_im * lane_sin
            im = odd_im * lane_cos - odd_re * lane_sin
            for tile in range(2):
                columns = slice(tile * half, (tile + 1) * half)
                chi_re = even_re - re if tile else even_re + re
                chi_im = even_im - im if tile else even_im + im
                own_col = lanes + tile * half >= dx
                pro_re = prot_ref[frame, 0, rows, columns]
                pro_im = prot_ref[frame, 1, rows, columns]
                obj_re = obj_ref[frame, 0, rows, columns]
                obj_im = obj_ref[frame, 1, rows, columns]
                for part, value in enumerate(
                    (pro_re * chi_re + pro_im * chi_im, pro_re * chi_im - pro_im * chi_re)
                ):
                    own = value
                    pieces = []
                    if row < margin:
                        own = jnp.where(own_row, value, 0.0)
                        other = jnp.where(own_row, 0.0, value)
                        pieces.append(("b", jnp.where(own_col, other, 0.0)))
                        pieces.append(("c", jnp.where(own_col, 0.0, other)))
                    pieces.append(("t", jnp.where(own_col, own, 0.0)))
                    pieces.append(("r", jnp.where(own_col, 0.0, own)))
                    for name, piece in pieces:
                        key = (name, part, tile)
                        total[key] = piece if frame == 0 else total[key] + piece
                for index, value in enumerate(
                    (
                        obj_re * chi_re + obj_im * chi_im,
                        obj_re * chi_im - obj_im * chi_re,
                        obj_re * obj_re + obj_im * obj_im,
                    )
                ):
                    twice[frame, index, tile, row : row + step] = value
                    twice[frame, index, tile, side + row : side + row + step] = value
        packed, lane = places[row]
        for part in range(2):
            gt_ref[part, rows, 0:half] = total["t", part, 0]
            gt_ref[part, rows, half:side] = total["t", part, 1]
            gr_ref[part, rows] = total["r", part, 0]
            gr_ref[part, side + packed : side + packed + 8, lane : lane + extra] = total["r", part, 1][:, 0:extra]
            if row < margin:
                gz_ref[part, rows] = total["b", part, 0]
                gz_ref[part, margin + row : margin + row + step] = total["b", part, 1]
                gr_ref[part, wide + row : wide + row + step] = total["c", part, 0]
                base = wide + margin + packed
                gr_ref[part, base : base + 8, lane : lane + extra] = total["c", part, 1][:, 0:extra]

    depth = qs_ref.shape[2]
    step = min(32, depth)
    lanes = lax.broadcasted_iota(jnp.int32, (step, half), 1)
    for row in range(0, side, step):
        for index in range(3):
            sums = None
            for frame in range(frames):
                dy = pos_ref[0, frame]
                dx = pos_ref[1, frame]
                pair = turned(
                    lambda tile: twice[frame, index, tile, pl.ds(dy + row, step), :], dx, half, lanes
                )
                sums = pair if sums is None else (sums[0] + pair[0], sums[1] + pair[1])
            place = slice(row % depth, row % depth + step)
            qs_ref[row // depth, index, place, 0:half] = sums[0]
            qs_ref[row // depth, index, place, half:side] = sums[1]


def finish_kernel(max_ref, tile_ref, grad_ref, right_ref, down_ref, corner_ref, out_ref):
    side = tile_ref.shape[1]
    half = side // 2
    margin = down_ref.shape[1] // 2
    extra = margin - half
    scale = 1.0 / max_ref[0, 0]
    step = 8
    for row, packed, lane in pack_extra(side, extra, half):
        place = slice(row, row + step)
        for part in range(2):
            one = grad_ref[part, place, 0:half] + right_ref[part, place]
            two = grad_ref[part, place, half:side]
            piece = right_ref[part, side + packed : side + packed + 8, lane : lane + extra]
            if row < margin:
                one = one + down_ref[part, place] + corner_ref[part, place]
                two = two + down_ref[part, margin + row : margin + row + step]
                piece = piece + corner_ref[part, margin + packed : margin + packed + 8, lane : lane + extra]
            out_ref[part, place, 0:half] = tile_ref[part, place, 0:half] + one * scale
            out_ref[part, place, half:side] = tile_ref[part, place, half:side] + two * scale
            out_ref[part, place, half:margin] += piece * scale


def body(object_field, probe_field, measured, positions):
    side = probe_field.shape[1]
    half = side // 2
    margin = HALO
    extra = margin - half
    frames = measured.shape[0]
    n_row, n_col = lax.axis_size("row"), lax.axis_size("col")
    fwd_right, fwd_left, inv_right, inv_left, lane_tw, row_tw = tables(side)
    wide = side + side * extra // half
    tall = margin + margin * extra // half

    below, corner, right = pl.pallas_call(
        pack_kernel,
        out_shape=(f32(2, 2 * margin, half), f32(2, tall, half), f32(2, wide, half)),
        in_specs=[VMEM],
        out_specs=(VMEM,) * 3,
        cost_estimate=cost(10**6, 2 * 10**6),
        compiler_params=PARAMS,
    )(object_field)
    below = shifted(below, "row", -1)
    corner = diagonal(corner)
    right = shifted(right, "col", -1)
    places = positions.T
    prot, ampl = pl.pallas_call(
        prepare_kernel,
        out_shape=(f32(frames, 2, side, side), f32(frames, side, side)),
        in_specs=[SMEM, VMEM, VMEM],
        out_specs=(VMEM, VMEM),
        scratch_shapes=[pltpu.VMEM((2, 2, 2 * side, half), jnp.float32)],
        cost_estimate=cost(3 * 10**9, 6 * 10**6),
        compiler_params=PARAMS,
    )(places, probe_field, measured)
    depth = side // n_col
    g_tile, g_right, g_down, sums, largest = pl.pallas_call(
        frame_kernel,
        out_shape=(
            f32(2, side, side),
            f32(2, wide + tall, half),
            f32(2, 2 * margin, half),
            f32(n_col, 3, depth, side),
            f32(1, 1),
        ),
        in_specs=[SMEM] + [VMEM] * 12,
        out_specs=(VMEM,) * 4 + (SMEM,),
        scratch_shapes=[
            pltpu.VMEM((2, side, half), jnp.float32),
            pltpu.VMEM((2, margin, half), jnp.float32),
            pltpu.VMEM((frames, 2, side, side), jnp.float32),
            pltpu.VMEM((2 * frames, side, 3 * side), BF16),
            pltpu.VMEM((2 * frames, 3 * side, side), BF16),
            pltpu.VMEM((2 * frames, side, side), jnp.float32),
            pltpu.VMEM((frames, 3, 2, 2 * side, half), jnp.float32),
        ],
        cost_estimate=cost(6 * 10**9, 12 * 10**6),
        compiler_params=PARAMS,
    )(
        places, object_field, right, below, corner, prot, ampl,
        fwd_right, fwd_left, inv_right, inv_left, lane_tw, row_tw,
    )

    from_above = shifted(g_down, "row", 1)
    part = jnp.sum(lax.all_to_all(sums, "col", 0, 0), 0)
    g_right, part, from_above = lax.optimization_barrier((g_right, part, from_above))
    from_left = shifted(g_right, "col", 1)
    part = row_sum(part)
    old = lax.dynamic_slice_in_dim(probe_field, lax.axis_index("col") * depth, depth, 1)
    new = old + part[:2] / (part[2] + 1.0)
    new, from_left = lax.optimization_barrier((new, from_left))
    new = lax.all_to_all(jnp.broadcast_to(new, (n_col,) + new.shape), "col", 0, 0)
    from_corner = shifted(from_left[:, wide:], "row", 1)
    new_probe = new.transpose(1, 0, 2, 3).reshape(2, side, side)
    new_object = pl.pallas_call(
        finish_kernel,
        out_shape=f32(2, side, side),
        in_specs=[SMEM] + [VMEM] * 5,
        out_specs=VMEM,
        cost_estimate=cost(10**6, 4 * 10**6),
        compiler_params=PARAMS,
    )(largest, object_field, g_tile, from_left, from_above, from_corner)
    return (new_object, new_probe)


def solution(mesh):
    in_specs = (P(None, "row", "col"), P(), P("row", "col", None), P("row", "col"))
    out_specs = (P(None, "row", "col"), P())
    return jax.shard_map(body, mesh=mesh, in_specs=in_specs, out_specs=out_specs, check_vma=False)
```

```python
import math

import jax
import jax.numpy as jnp
import numpy as np
from jax import lax
from jax.experimental import pallas as pl
from jax.experimental.pallas import tpu as pltpu
from jax.sharding import PartitionSpec as P

HALO = 160
VMEM = pl.BlockSpec(memory_space=pltpu.VMEM)
SMEM = pl.BlockSpec(memory_space=pltpu.SMEM)
PARAMS = pltpu.CompilerParams(vmem_limit_bytes=24 * 1024 * 1024)
BF16 = jnp.bfloat16


def shifted(value, axis, steps):
    count = lax.axis_size(axis)
    initial, last = (max(0, -steps), min(count, count - steps))
    return lax.ppermute(value, axis, [(source, source + steps) for source in range(initial, last)])


def row_terms(value):
    rows = lax.axis_size("row")
    if rows != 4:
        return [lax.psum(value, "row")]
    return [value] + [
        lax.ppermute(value, "row", [(row, row ^ step) for row in range(rows)]) for step in (1, 2, 3)
    ]


def f32(*shape):
    return jax.ShapeDtypeStruct(shape, jnp.float32)


def cost(flops, moved):
    return pl.CostEstimate(flops=flops, bytes_accessed=moved, transcendentals=0)


def tables(side):
    half = side // 2
    index = np.arange(half)
    angle = 2.0 * math.pi / half * (np.outer(index, index) % half)
    cos = np.cos(angle) / math.sqrt(side)
    sin = -np.sin(angle) / math.sqrt(side)
    matrix = np.block([[cos, sin], [-sin, cos]])
    high = matrix.astype(BF16)
    low = (matrix - high.astype(np.float64)).astype(BF16)
    turn = -2.0 * math.pi / side * index
    twiddle = np.stack([np.cos(turn), np.sin(turn)]).astype(np.float32)
    lanes = np.ascontiguousarray(np.broadcast_to(twiddle[:, None, :], (2, 8, half)))
    rows = np.ascontiguousarray(np.broadcast_to(twiddle[:, :, None], (2, half, half)))
    return (
        np.concatenate([high, high, low], 0),
        np.concatenate([high.T, high.T, low.T], 1),
        np.concatenate([high.T, high.T, low.T], 0),
        np.concatenate([high, high, low], 1),
        lanes,
        rows,
    )


def dot(left, right):
    return jnp.dot(left, right, preferred_element_type=jnp.float32)


def halves(value):
    high = value.astype(BF16)
    low = (value - high.astype(jnp.float32)).astype(BF16)
    return high, low


def pack_extra(rows, extra, width):
    per = width // extra
    for group in range(rows // 8):
        yield group * 8, group // per * 8, group % per * extra


def pack_kernel(tile_ref, near_ref, far_ref, right_ref):
    side = tile_ref.shape[1]
    half = side // 2
    margin = far_ref.shape[1]
    extra = margin - half
    near_ref[:, 0:margin, :] = tile_ref[:, 0:margin, 0:half]
    far_ref[...] = tile_ref[:, 0:margin, half:]
    right_ref[:, 0:side, :] = tile_ref[:, :, 0:half]
    for row, packed, lane in pack_extra(side, extra, half):
        piece = tile_ref[:, row : row + 8, half:margin]
        right_ref[:, side + packed : side + packed + 8, lane : lane + extra] = piece
        if row < margin:
            near_ref[:, margin + packed : margin + packed + 8, lane : lane + extra] = piece


def peak_kernel(probe_ref, meas_ref, out_ref):
    re, im = probe_ref[0], probe_ref[1]
    top = jnp.max(re * re + im * im, axis=(0, 1), keepdims=True)
    out_ref[0] = jnp.broadcast_to(top, out_ref.shape[1:])
    out_ref[1] = meas_ref[0, 0:8, 0 : out_ref.shape[2]]


def turned(load, steps, half, lanes):
    within = lax.rem(steps, half)
    first = lax.rem(lax.div(steps, half), 2)
    back = lax.rem(half - within, half)
    one = pltpu.roll(load(first), back, 1)
    two = pltpu.roll(load(1 - first), back, 1)
    stay = lanes < half - within
    return jnp.where(stay, one, two), jnp.where(stay, two, one)


def prepare_kernel(pos_ref, probe_ref, meas_ref, prot_ref, sorted_ref, twice):
    frames, side = meas_ref.shape[0], meas_ref.shape[1]
    half = side // 2
    for part in range(2):
        for tile in range(2):
            piece = probe_ref[part, :, tile * half : (tile + 1) * half]
            twice[part, tile, 0:side] = piece
            twice[part, tile, side : 2 * side] = piece
    step = 64
    lanes = lax.broadcasted_iota(jnp.int32, (step, half), 1)
    rows = lax.broadcasted_iota(jnp.int32, (side, side), 0)
    cols = lax.broadcasted_iota(jnp.int32, (side, side), 1)
    sort = jnp.where(rows == jnp.where(cols < half, 2 * cols, 2 * cols - side + 1), 1.0, 0.0).astype(BF16)
    unsort = jnp.where(cols == jnp.where(rows < half, 2 * rows, 2 * rows - side + 1), 1.0, 0.0).astype(BF16)

    @pl.loop(0, frames)
    def _(frame):
        dy = pos_ref[0, frame]
        dx = pos_ref[1, frame]
        for part in range(2):
            for row in range(0, side, step):
                one, two = turned(
                    lambda tile: twice[part, tile, pl.ds(side - dy + row, step), :], side - dx, half, lanes
                )
                prot_ref[frame, part, row : row + step, 0:half] = one
                prot_ref[frame, part, row : row + step, half:side] = two
        value = meas_ref[frame]
        total = None
        for _ in range(3):
            piece = value.astype(BF16)
            value = value - piece.astype(jnp.float32)
            term = dot(dot(unsort, piece).astype(BF16), sort)
            total = term if total is None else total + term
        sorted_ref[frame] = total


def frame_kernel(
    pos_ref, tile_ref, right_ref, near_ref, far_ref, corner_ref, prot_ref, meas_ref,
    fwd_right, fwd_left, inv_right, inv_left, lane_ref, row_ref,
    gt_ref, gr_ref, gz_ref, qs_ref,
    right_extra, corner_extra, obj_ref, left_in, right_in, mid, twice,
):
    frames, side = meas_ref.shape[0], meas_ref.shape[1]
    half = side // 2
    margin = far_ref.shape[1]
    wide = right_ref.shape[1]
    extra = margin - half
    for row, packed, lane in pack_extra(side, extra, half):
        right_extra[:, row : row + 8, 0:extra] = right_ref[:, side + packed : side + packed + 8, lane : lane + extra]
        if row < margin:
            corner_extra[:, row : row + 8, 0:extra] = corner_ref[
                :, margin + packed : margin + packed + 8, lane : lane + extra
            ]
    lane_cos, lane_sin = lane_ref[0, 0:1], lane_ref[1, 0:1]

    def store_left(where, rows, tile, value):
        high, low = halves(value)
        lane = tile * half
        left_in[where, rows, lane : lane + half] = high
        left_in[where, rows, side + lane : side + lane + half] = low
        left_in[where, rows, 2 * side + lane : 2 * side + lane + half] = high

    def store_right(where, row, count, columns, value):
        high, low = halves(value)
        right_in[where, row : row + count, columns] = high
        right_in[where, side + row : side + row + count, columns] = low
        right_in[where, 2 * side + row : 2 * side + row + count, columns] = high

    step = 32
    lanes = lax.broadcasted_iota(jnp.int32, (step, half), 1)
    row_in = lax.broadcasted_iota(jnp.int32, (step, half), 0)
    for frame in range(frames):
        dy = pos_ref[0, frame]
        dx = pos_ref[1, frame]
        own_col = (lanes >= dx, lanes + half >= dx)
        for row in range(0, side, step):
            rows = slice(row, row + step)
            own_row = row_in + row >= dy
            wave = []
            for tile in range(2):
                columns = slice(tile * half, (tile + 1) * half)
                obj = []
                for part in range(2):
                    right = right_extra[part, rows] if tile else right_ref[part, rows]
                    value = jnp.where(own_col[tile], tile_ref[part, rows, columns], right)
                    if row < margin:
                        below = far_ref[part, rows] if tile else near_ref[part, rows]
                        corner = corner_extra[part, rows] if tile else corner_ref[part, rows]
                        value = jnp.where(own_row, value, jnp.where(own_col[tile], below, corner))
                    obj_ref[frame, part, rows, columns] = value
                    obj.append(value)
                pro_re = prot_ref[frame, 0, rows, columns]
                pro_im = prot_ref[frame, 1, rows, columns]
                wave.append((pro_re * obj[0] - pro_im * obj[1], pro_re * obj[1] + pro_im * obj[0]))
            (re0, im0), (re1, im1) = wave
            store_left(2 * frame, rows, 0, re0 + re1)
            store_left(2 * frame, rows, 1, im0 + im1)
            re, im = re0 - re1, im0 - im1
            store_left(2 * frame + 1, rows, 0, re * lane_cos - im * lane_sin)
            store_left(2 * frame + 1, rows, 1, re * lane_sin + im * lane_cos)
        for which in range(2):
            mid[2 * frame + which] = dot(left_in[2 * frame + which], fwd_right[...])

    for frame in range(frames):
        for row in range(0, half, step):
            top, low = slice(row, row + step), slice(half + row, half + row + step)
            row_cos, row_sin = row_ref[0, top], row_ref[1, top]
            for which in range(2):
                columns = slice(which * half, (which + 1) * half)
                top_re, top_im = mid[2 * frame + which, top, 0:half], mid[2 * frame + which, top, half:side]
                low_re, low_im = mid[2 * frame + which, low, 0:half], mid[2 * frame + which, low, half:side]
                store_right(2 * frame, row, step, columns, top_re + low_re)
                store_right(2 * frame, half + row, step, columns, top_im + low_im)
                re, im = top_re - low_re, top_im - low_im
                store_right(2 * frame + 1, row, step, columns, re * row_cos - im * row_sin)
                store_right(2 * frame + 1, half + row, step, columns, re * row_sin + im * row_cos)
        for which in range(2):
            mid[2 * frame + which] = dot(fwd_left[...], right_in[2 * frame + which])

    for frame in range(frames):
        for which in range(2):
            for row in range(0, half, step):
                re = mid[2 * frame + which, row : row + step]
                im = mid[2 * frame + which, half + row : half + row + step]
                ampl = meas_ref[frame, which * half + row : which * half + row + step]
                factor = ampl * lax.rsqrt(jnp.maximum(re * re + im * im, 0.25)) - 1.0
                store_right(2 * frame + which, row, step, slice(0, side), factor * re)
                store_right(2 * frame + which, half + row, step, slice(0, side), factor * im)
            mid[2 * frame + which] = dot(inv_left[...], right_in[2 * frame + which])

    for frame in range(frames):
        for row in range(0, half, step):
            top, low = slice(row, row + step), slice(half + row, half + row + step)
            row_cos, row_sin = row_ref[0, top], row_ref[1, top]
            for which in range(2):
                columns = slice(which * half, (which + 1) * half)
                even_re, even_im = mid[2 * frame, top, columns], mid[2 * frame, low, columns]
                odd_re, odd_im = mid[2 * frame + 1, top, columns], mid[2 * frame + 1, low, columns]
                re = odd_re * row_cos + odd_im * row_sin
                im = odd_im * row_cos - odd_re * row_sin
                store_left(2 * frame + which, top, 0, even_re + re)
                store_left(2 * frame + which, top, 1, even_im + im)
                store_left(2 * frame + which, low, 0, even_re - re)
                store_left(2 * frame + which, low, 1, even_im - im)
        for which in range(2):
            mid[2 * frame + which] = dot(left_in[2 * frame + which], inv_right[...])

    step = 8
    lanes = lax.broadcasted_iota(jnp.int32, (step, half), 1)
    row_in = lax.broadcasted_iota(jnp.int32, (step, half), 0)
    places = {row: (packed, lane) for row, packed, lane in pack_extra(side, extra, half)}
    for row in range(0, side, step):
        rows = slice(row, row + step)
        total = {}
        for frame in range(frames):
            dy = pos_ref[0, frame]
            dx = pos_ref[1, frame]
            own_row = row_in + row >= dy
            even_re, even_im = mid[2 * frame, rows, 0:half], mid[2 * frame, rows, half:side]
            odd_re, odd_im = mid[2 * frame + 1, rows, 0:half], mid[2 * frame + 1, rows, half:side]
            re = odd_re * lane_cos + odd_im * lane_sin
            im = odd_im * lane_cos - odd_re * lane_sin
            for tile in range(2):
                columns = slice(tile * half, (tile + 1) * half)
                chi_re = even_re - re if tile else even_re + re
                chi_im = even_im - im if tile else even_im + im
                own_col = lanes + tile * half >= dx
                pro_re = prot_ref[frame, 0, rows, columns]
                pro_im = prot_ref[frame, 1, rows, columns]
                obj_re = obj_ref[frame, 0, rows, columns]
                obj_im = obj_ref[frame, 1, rows, columns]
                for part, value in enumerate(
                    (pro_re * chi_re + pro_im * chi_im, pro_re * chi_im - pro_im * chi_re)
                ):
                    own = value
                    pieces = []
                    if row < margin:
                        own = jnp.where(own_row, value, 0.0)
                        other = jnp.where(own_row, 0.0, value)
                        pieces.append(("b", jnp.where(own_col, other, 0.0)))
                        pieces.append(("c", jnp.where(own_col, 0.0, other)))
                    pieces.append(("t", jnp.where(own_col, own, 0.0)))
                    pieces.append(("r", jnp.where(own_col, 0.0, own)))
                    for name, piece in pieces:
                        key = (name, part, tile)
                        total[key] = piece if frame == 0 else total[key] + piece
                for index, value in enumerate(
                    (
                        obj_re * chi_re + obj_im * chi_im,
                        obj_re * chi_im - obj_im * chi_re,
                        obj_re * obj_re + obj_im * obj_im,
                    )
                ):
                    twice[frame, index, tile, row : row + step] = value
                    twice[frame, index, tile, side + row : side + row + step] = value
        packed, lane = places[row]
        for part in range(2):
            gt_ref[part, rows, 0:half] = total["t", part, 0]
            gt_ref[part, rows, half:side] = total["t", part, 1]
            gr_ref[part, rows] = total["r", part, 0]
            gr_ref[part, side + packed : side + packed + 8, lane : lane + extra] = total["r", part, 1][:, 0:extra]
            if row < margin:
                gz_ref[part, rows] = total["b", part, 0]
                gz_ref[part, margin + row : margin + row + step] = total["b", part, 1]
                gr_ref[part, wide + row : wide + row + step] = total["c", part, 0]
                base = wide + margin + packed
                gr_ref[part, base : base + 8, lane : lane + extra] = total["c", part, 1][:, 0:extra]

    depth = qs_ref.shape[2]
    step = min(32, depth)
    lanes = lax.broadcasted_iota(jnp.int32, (step, half), 1)
    for row in range(0, side, step):
        for index in range(3):
            sums = None
            for frame in range(frames):
                dy = pos_ref[0, frame]
                dx = pos_ref[1, frame]
                pair = turned(
                    lambda tile: twice[frame, index, tile, pl.ds(dy + row, step), :], dx, half, lanes
                )
                sums = pair if sums is None else (sums[0] + pair[0], sums[1] + pair[1])
            place = slice(row % depth, row % depth + step)
            qs_ref[row // depth, index, place, 0:half] = sums[0]
            qs_ref[row // depth, index, place, half:side] = sums[1]


def update_kernel(old_ref, *refs):
    terms, out_ref = refs[:-1], refs[-1]

    def total(index):
        values = [term[index] for term in terms]
        while len(values) > 1:
            values = [values[at] + values[at + 1] for at in range(0, len(values), 2)]
        return values[0]

    weight = total(2) + 1.0
    for part in range(2):
        value = old_ref[part] + total(part) / weight
        for copy in range(out_ref.shape[0]):
            out_ref[copy, part] = value


def finish_kernel(peak_ref, tile_ref, grad_ref, right_ref, down_ref, corner_ref, out_ref):
    side = tile_ref.shape[1]
    half = side // 2
    margin = down_ref.shape[1] // 2
    extra = margin - half
    largest = peak_ref[0]
    step = 8
    for row, packed, lane in pack_extra(side, extra, half):
        place = slice(row, row + step)
        for part in range(2):
            one = grad_ref[part, place, 0:half] + right_ref[part, place]
            two = grad_ref[part, place, half:side]
            piece = right_ref[part, side + packed : side + packed + 8, lane : lane + extra]
            if row < margin:
                one = one + down_ref[part, place] + corner_ref[part, place]
                two = two + down_ref[part, margin + row : margin + row + step]
                piece = piece + corner_ref[part, margin + packed : margin + packed + 8, lane : lane + extra]
            out_ref[part, place, 0:half] = tile_ref[part, place, 0:half] + one / largest
            out_ref[part, place, half:side] = tile_ref[part, place, half:side] + two / largest
            out_ref[part, place, half:margin] += piece / largest[:, 0:extra]


def body(object_field, probe_field, measured, positions):
    side = probe_field.shape[1]
    half = side // 2
    margin = HALO
    extra = margin - half
    frames = measured.shape[0]
    n_row, n_col = lax.axis_size("row"), lax.axis_size("col")
    fwd_right, fwd_left, inv_right, inv_left, lane_tw, row_tw = tables(side)
    wide = side + side * extra // half
    tall = margin + margin * extra // half

    near, far, right = pl.pallas_call(
        pack_kernel,
        out_shape=(f32(2, tall, half), f32(2, margin, half), f32(2, wide, half)),
        in_specs=[VMEM],
        out_specs=(VMEM,) * 3,
        cost_estimate=cost(10**6, 2 * 10**6),
        compiler_params=PARAMS,
    )(object_field)
    near = shifted(near, "row", -1)
    far = shifted(far, "row", -1)
    right = shifted(right, "col", -1)
    peak = pl.pallas_call(
        peak_kernel,
        out_shape=f32(2, 8, half),
        in_specs=[VMEM, VMEM],
        out_specs=VMEM,
        cost_estimate=cost(10**6, 2 * 10**6),
        compiler_params=PARAMS,
    )(probe_field, measured)
    near, peak = lax.optimization_barrier((near, peak))
    corner = shifted(near, "col", -1)
    places = positions.T
    prot, ampl = pl.pallas_call(
        prepare_kernel,
        out_shape=(f32(frames, 2, side, side), f32(frames, side, side)),
        in_specs=[SMEM, VMEM, VMEM],
        out_specs=(VMEM, VMEM),
        scratch_shapes=[pltpu.VMEM((2, 2, 2 * side, half), jnp.float32)],
        cost_estimate=cost(3 * 10**9, 6 * 10**6),
        compiler_params=PARAMS,
    )(places, probe_field, measured)
    depth = side // n_col
    g_tile, g_right, g_down, sums = pl.pallas_call(
        frame_kernel,
        out_shape=(
            f32(2, side, side),
            f32(2, wide + tall, half),
            f32(2, 2 * margin, half),
            f32(n_col, 3, depth, side),
        ),
        in_specs=[SMEM] + [VMEM] * 13,
        out_specs=(VMEM,) * 4,
        scratch_shapes=[
            pltpu.VMEM((2, side, half), jnp.float32),
            pltpu.VMEM((2, margin, half), jnp.float32),
            pltpu.VMEM((frames, 2, side, side), jnp.float32),
            pltpu.VMEM((2 * frames, side, 3 * side), BF16),
            pltpu.VMEM((2 * frames, 3 * side, side), BF16),
            pltpu.VMEM((2 * frames, side, side), jnp.float32),
            pltpu.VMEM((frames, 3, 2, 2 * side, half), jnp.float32),
        ],
        cost_estimate=cost(6 * 10**9, 12 * 10**6),
        compiler_params=PARAMS,
    )(
        places, object_field, right, near, far, corner, prot, ampl,
        fwd_right, fwd_left, inv_right, inv_left, lane_tw, row_tw,
    )

    from_above = shifted(g_down, "row", 1)
    part = jnp.sum(lax.all_to_all(sums, "col", 0, 0), 0)
    g_right, part, from_above = lax.optimization_barrier((g_right, part, from_above))
    from_left = shifted(g_right, "col", 1)
    old = lax.dynamic_slice_in_dim(probe_field, lax.axis_index("col") * depth, depth, 1)
    terms = row_terms(part)
    new = pl.pallas_call(
        update_kernel,
        out_shape=f32(n_col, 2, depth, side),
        in_specs=[VMEM] * (1 + len(terms)),
        out_specs=VMEM,
        cost_estimate=cost(10**6, 10**6),
        compiler_params=PARAMS,
    )(old, *terms)
    new, from_left = lax.optimization_barrier((new, from_left))
    new = lax.all_to_all(new, "col", 0, 0)
    from_corner = shifted(from_left[:, wide:], "row", 1)
    new_probe = new.transpose(1, 0, 2, 3).reshape(2, side, side)
    new_object = pl.pallas_call(
        finish_kernel,
        out_shape=f32(2, side, side),
        in_specs=[VMEM] * 6,
        out_specs=VMEM,
        cost_estimate=cost(10**6, 4 * 10**6),
        compiler_params=PARAMS,
    )(peak, object_field, g_tile, from_left, from_above, from_corner)
    return (new_object, new_probe)


def solution(mesh):
    in_specs = (P(None, "row", "col"), P(), P("row", "col", None), P("row", "col"))
    out_specs = (P(None, "row", "col"), P())
    return jax.shard_map(body, mesh=mesh, in_specs=in_specs, out_specs=out_specs, check_vma=False)
```

```python
import math

import jax
import jax.numpy as jnp
import numpy as np
from jax import lax
from jax.experimental import pallas as pl
from jax.experimental.pallas import tpu as pltpu
from jax.sharding import PartitionSpec as P

HALO = 160
VMEM = pl.BlockSpec(memory_space=pltpu.VMEM)
SMEM = pl.BlockSpec(memory_space=pltpu.SMEM)
PARAMS = pltpu.CompilerParams(vmem_limit_bytes=24 * 1024 * 1024)
BF16 = jnp.bfloat16


def shifted(value, axis, steps):
    count = lax.axis_size(axis)
    initial, last = (max(0, -steps), min(count, count - steps))
    return lax.ppermute(value, axis, [(source, source + steps) for source in range(initial, last)])


def diagonal(value):
    rows, cols = lax.axis_size("row"), lax.axis_size("col")
    pairs = [
        (row * cols + col, (row + 1) * cols + col + 1) for row in range(rows - 1) for col in range(cols - 1)
    ]
    return lax.ppermute(value, ("row", "col"), pairs)


def row_terms(value):
    rows = lax.axis_size("row")
    if rows != 4:
        return [lax.psum(value, "row")]
    three, two, one = (
        lax.ppermute(value, "row", [(row, row ^ step) for row in range(rows)]) for step in (3, 2, 1)
    )
    return [two, three, value, one]


def f32(*shape):
    return jax.ShapeDtypeStruct(shape, jnp.float32)


def cost(flops, moved):
    return pl.CostEstimate(flops=flops, bytes_accessed=moved, transcendentals=0)


def tables(side):
    half = side // 2
    index = np.arange(half)
    angle = 2.0 * math.pi / half * (np.outer(index, index) % half)
    cos = np.cos(angle) / math.sqrt(side)
    sin = -np.sin(angle) / math.sqrt(side)
    matrix = np.block([[cos, sin], [-sin, cos]])
    high = matrix.astype(BF16)
    low = (matrix - high.astype(np.float64)).astype(BF16)
    turn = -2.0 * math.pi / side * index
    twiddle = np.stack([np.cos(turn), np.sin(turn)]).astype(np.float32)
    lanes = np.ascontiguousarray(np.broadcast_to(twiddle[:, None, :], (2, 8, half)))
    rows = np.ascontiguousarray(np.broadcast_to(twiddle[:, :, None], (2, half, half)))
    return (
        np.concatenate([high, high, low], 0),
        np.concatenate([high.T, high.T, low.T], 1),
        np.concatenate([high.T, high.T, low.T], 0),
        np.concatenate([high, high, low], 1),
        lanes,
        rows,
    )


def dot(left, right):
    return jnp.dot(left, right, preferred_element_type=jnp.float32)


def halves(value):
    high = value.astype(BF16)
    low = (value - high.astype(jnp.float32)).astype(BF16)
    return high, low


def pack_extra(rows, extra, width):
    per = width // extra
    for group in range(rows // 8):
        yield group * 8, group // per * 8, group % per * extra


def pack_kernel(tile_ref, near_ref, far_ref, right_ref):
    side = tile_ref.shape[1]
    half = side // 2
    margin = far_ref.shape[1]
    extra = margin - half
    near_ref[:, 0:margin, :] = tile_ref[:, 0:margin, 0:half]
    far_ref[...] = tile_ref[:, 0:margin, half:]
    right_ref[:, 0:side, :] = tile_ref[:, :, 0:half]
    for row, packed, lane in pack_extra(side, extra, half):
        piece = tile_ref[:, row : row + 8, half:margin]
        right_ref[:, side + packed : side + packed + 8, lane : lane + extra] = piece
        if row < margin:
            near_ref[:, margin + packed : margin + packed + 8, lane : lane + extra] = piece


def peak_kernel(probe_ref, meas_ref, out_ref):
    re, im = probe_ref[0], probe_ref[1]
    top = jnp.max(re * re + im * im, axis=(0, 1), keepdims=True)
    out_ref[0] = jnp.broadcast_to(top, out_ref.shape[1:])
    out_ref[1] = meas_ref[0, 0:8, 0 : out_ref.shape[2]]


def turned(load, steps, half, lanes):
    within = lax.rem(steps, half)
    first = lax.rem(lax.div(steps, half), 2)
    back = lax.rem(half - within, half)
    one = pltpu.roll(load(first), back, 1)
    two = pltpu.roll(load(1 - first), back, 1)
    stay = lanes < half - within
    return jnp.where(stay, one, two), jnp.where(stay, two, one)


def prepare_kernel(pos_ref, probe_ref, meas_ref, prot_ref, sorted_ref, twice):
    frames, side = meas_ref.shape[0], meas_ref.shape[1]
    half = side // 2
    for part in range(2):
        for tile in range(2):
            piece = probe_ref[part, :, tile * half : (tile + 1) * half]
            twice[part, tile, 0:side] = piece
            twice[part, tile, side : 2 * side] = piece
    step = 64
    lanes = lax.broadcasted_iota(jnp.int32, (step, half), 1)
    rows = lax.broadcasted_iota(jnp.int32, (side, side), 0)
    cols = lax.broadcasted_iota(jnp.int32, (side, side), 1)
    sort = jnp.where(rows == jnp.where(cols < half, 2 * cols, 2 * cols - side + 1), 1.0, 0.0).astype(BF16)
    unsort = jnp.where(cols == jnp.where(rows < half, 2 * rows, 2 * rows - side + 1), 1.0, 0.0).astype(BF16)

    @pl.loop(0, frames)
    def _(frame):
        dy = pos_ref[0, frame]
        dx = pos_ref[1, frame]
        for part in range(2):
            for row in range(0, side, step):
                one, two = turned(
                    lambda tile: twice[part, tile, pl.ds(side - dy + row, step), :], side - dx, half, lanes
                )
                prot_ref[frame, part, row : row + step, 0:half] = one
                prot_ref[frame, part, row : row + step, half:side] = two
        value = meas_ref[frame]
        total = None
        for _ in range(3):
            piece = value.astype(BF16)
            value = value - piece.astype(jnp.float32)
            term = dot(dot(unsort, piece).astype(BF16), sort)
            total = term if total is None else total + term
        sorted_ref[frame] = total


def frame_kernel(
    pos_ref, tile_ref, right_ref, near_ref, far_ref, corner_ref, prot_ref, meas_ref,
    fwd_right, fwd_left, inv_right, inv_left, lane_ref, row_ref,
    gt_ref, gr_ref, gz_ref, gc_ref, qs_ref,
    right_extra, corner_extra, obj_ref, left_in, right_in, mid, twice,
):
    frames, side = meas_ref.shape[0], meas_ref.shape[1]
    half = side // 2
    margin = far_ref.shape[1]
    extra = margin - half
    for row, packed, lane in pack_extra(side, extra, half):
        right_extra[:, row : row + 8, 0:extra] = right_ref[:, side + packed : side + packed + 8, lane : lane + extra]
        if row < margin:
            corner_extra[:, row : row + 8, 0:extra] = corner_ref[
                :, margin + packed : margin + packed + 8, lane : lane + extra
            ]
    lane_cos, lane_sin = lane_ref[0, 0:1], lane_ref[1, 0:1]

    def store_left(where, rows, tile, value):
        high, low = halves(value)
        lane = tile * half
        left_in[where, rows, lane : lane + half] = high
        left_in[where, rows, side + lane : side + lane + half] = low
        left_in[where, rows, 2 * side + lane : 2 * side + lane + half] = high

    def store_right(where, row, count, columns, value):
        high, low = halves(value)
        right_in[where, row : row + count, columns] = high
        right_in[where, side + row : side + row + count, columns] = low
        right_in[where, 2 * side + row : 2 * side + row + count, columns] = high

    step = 32
    lanes = lax.broadcasted_iota(jnp.int32, (step, half), 1)
    row_in = lax.broadcasted_iota(jnp.int32, (step, half), 0)
    for frame in range(frames):
        dy = pos_ref[0, frame]
        dx = pos_ref[1, frame]
        own_col = (lanes >= dx, lanes + half >= dx)
        for row in range(0, side, step):
            rows = slice(row, row + step)
            own_row = row_in + row >= dy
            wave = []
            for tile in range(2):
                columns = slice(tile * half, (tile + 1) * half)
                obj = []
                for part in range(2):
                    right = right_extra[part, rows] if tile else right_ref[part, rows]
                    value = jnp.where(own_col[tile], tile_ref[part, rows, columns], right)
                    if row < margin:
                        below = far_ref[part, rows] if tile else near_ref[part, rows]
                        corner = corner_extra[part, rows] if tile else corner_ref[part, rows]
                        value = jnp.where(own_row, value, jnp.where(own_col[tile], below, corner))
                    obj_ref[frame, part, rows, columns] = value
                    obj.append(value)
                pro_re = prot_ref[frame, 0, rows, columns]
                pro_im = prot_ref[frame, 1, rows, columns]
                wave.append((pro_re * obj[0] - pro_im * obj[1], pro_re * obj[1] + pro_im * obj[0]))
            (re0, im0), (re1, im1) = wave
            store_left(2 * frame, rows, 0, re0 + re1)
            store_left(2 * frame, rows, 1, im0 + im1)
            re, im = re0 - re1, im0 - im1
            store_left(2 * frame + 1, rows, 0, re * lane_cos - im * lane_sin)
            store_left(2 * frame + 1, rows, 1, re * lane_sin + im * lane_cos)
        for which in range(2):
            mid[2 * frame + which] = dot(left_in[2 * frame + which], fwd_right[...])

    for frame in range(frames):
        for row in range(0, half, step):
            top, low = slice(row, row + step), slice(half + row, half + row + step)
            row_cos, row_sin = row_ref[0, top], row_ref[1, top]
            for which in range(2):
                columns = slice(which * half, (which + 1) * half)
                top_re, top_im = mid[2 * frame + which, top, 0:half], mid[2 * frame + which, top, half:side]
                low_re, low_im = mid[2 * frame + which, low, 0:half], mid[2 * frame + which, low, half:side]
                store_right(2 * frame, row, step, columns, top_re + low_re)
                store_right(2 * frame, half + row, step, columns, top_im + low_im)
                re, im = top_re - low_re, top_im - low_im
                store_right(2 * frame + 1, row, step, columns, re * row_cos - im * row_sin)
                store_right(2 * frame + 1, half + row, step, columns, re * row_sin + im * row_cos)
        for which in range(2):
            mid[2 * frame + which] = dot(fwd_left[...], right_in[2 * frame + which])

    for frame in range(frames):
        for which in range(2):
            for row in range(0, half, step):
                re = mid[2 * frame + which, row : row + step]
                im = mid[2 * frame + which, half + row : half + row + step]
                ampl = meas_ref[frame, which * half + row : which * half + row + step]
                factor = ampl * lax.rsqrt(jnp.maximum(re * re + im * im, 0.25)) - 1.0
                store_right(2 * frame + which, row, step, slice(0, side), factor * re)
                store_right(2 * frame + which, half + row, step, slice(0, side), factor * im)
            mid[2 * frame + which] = dot(inv_left[...], right_in[2 * frame + which])

    for frame in range(frames):
        for row in range(0, half, step):
            top, low = slice(row, row + step), slice(half + row, half + row + step)
            row_cos, row_sin = row_ref[0, top], row_ref[1, top]
            for which in range(2):
                columns = slice(which * half, (which + 1) * half)
                even_re, even_im = mid[2 * frame, top, columns], mid[2 * frame, low, columns]
                odd_re, odd_im = mid[2 * frame + 1, top, columns], mid[2 * frame + 1, low, columns]
                re = odd_re * row_cos + odd_im * row_sin
                im = odd_im * row_cos - odd_re * row_sin
                store_left(2 * frame + which, top, 0, even_re + re)
                store_left(2 * frame + which, top, 1, even_im + im)
                store_left(2 * frame + which, low, 0, even_re - re)
                store_left(2 * frame + which, low, 1, even_im - im)
        for which in range(2):
            mid[2 * frame + which] = dot(left_in[2 * frame + which], inv_right[...])

    step = 8
    lanes = lax.broadcasted_iota(jnp.int32, (step, half), 1)
    row_in = lax.broadcasted_iota(jnp.int32, (step, half), 0)
    places = {row: (packed, lane) for row, packed, lane in pack_extra(side, extra, half)}
    for row in range(0, side, step):
        rows = slice(row, row + step)
        total = {}
        for frame in range(frames):
            dy = pos_ref[0, frame]
            dx = pos_ref[1, frame]
            masks = []
            for tile in range(2):
                own_col = lanes + tile * half >= dx
                far_col = jnp.logical_not(own_col)
                if row < margin:
                    own_row = row_in + row >= dy
                    far_row = jnp.logical_not(own_row)
                    masks.append(
                        {"t": own_row & own_col, "r": own_row & far_col, "b": far_row & own_col, "c": far_row & far_col}
                    )
                else:
                    masks.append({"t": own_col, "r": far_col})
            even_re, even_im = mid[2 * frame, rows, 0:half], mid[2 * frame, rows, half:side]
            odd_re, odd_im = mid[2 * frame + 1, rows, 0:half], mid[2 * frame + 1, rows, half:side]
            re = odd_re * lane_cos + odd_im * lane_sin
            im = odd_im * lane_cos - odd_re * lane_sin
            for tile in range(2):
                columns = slice(tile * half, (tile + 1) * half)
                chi_re = even_re - re if tile else even_re + re
                chi_im = even_im - im if tile else even_im + im
                pro_re = prot_ref[frame, 0, rows, columns]
                pro_im = prot_ref[frame, 1, rows, columns]
                obj_re = obj_ref[frame, 0, rows, columns]
                obj_im = obj_ref[frame, 1, rows, columns]
                for part, value in enumerate(
                    (pro_re * chi_re + pro_im * chi_im, pro_re * chi_im - pro_im * chi_re)
                ):
                    for name, mask in masks[tile].items():
                        piece = jnp.where(mask, value, 0.0)
                        key = (name, part, tile)
                        total[key] = piece if frame == 0 else total[key] + piece
                for index, value in enumerate(
                    (
                        obj_re * chi_re + obj_im * chi_im,
                        obj_re * chi_im - obj_im * chi_re,
                        obj_re * obj_re + obj_im * obj_im,
                    )
                ):
                    twice[frame, index, tile, row : row + step] = value
                    if row < margin:
                        twice[frame, index, tile, side + row : side + row + step] = value
        packed, lane = places[row]
        for part in range(2):
            gt_ref[part, rows, 0:half] = total["t", part, 0]
            gt_ref[part, rows, half:side] = total["t", part, 1]
            gr_ref[part, rows] = total["r", part, 0]
            gr_ref[part, side + packed : side + packed + 8, lane : lane + extra] = total["r", part, 1][:, 0:extra]
            if row < margin:
                gz_ref[part, rows] = total["b", part, 0]
                gz_ref[part, margin + row : margin + row + step] = total["b", part, 1]
                gc_ref[part, rows] = total["c", part, 0]
                base = margin + packed
                gc_ref[part, base : base + 8, lane : lane + extra] = total["c", part, 1][:, 0:extra]

    depth = qs_ref.shape[2]
    step = min(32, depth)
    lanes = lax.broadcasted_iota(jnp.int32, (step, half), 1)
    for row in range(0, side, step):
        for index in range(3):
            sums = None
            for frame in range(frames):
                dy = pos_ref[0, frame]
                dx = pos_ref[1, frame]
                pair = turned(
                    lambda tile: twice[frame, index, tile, pl.ds(dy + row, step), :], dx, half, lanes
                )
                sums = pair if sums is None else (sums[0] + pair[0], sums[1] + pair[1])
            place = slice(row % depth, row % depth + step)
            qs_ref[row // depth, index, place, 0:half] = sums[0]
            qs_ref[row // depth, index, place, half:side] = sums[1]


def update_kernel(old_ref, *refs):
    terms, out_ref = refs[:-1], refs[-1]

    def total(index):
        values = [term[index] for term in terms]
        while len(values) > 1:
            values = [values[at] + values[at + 1] for at in range(0, len(values), 2)]
        return values[0]

    weight = total(2) + 1.0
    for part in range(2):
        value = old_ref[part] + total(part) / weight
        for copy in range(out_ref.shape[0]):
            out_ref[copy, part] = value


def finish_kernel(peak_ref, tile_ref, grad_ref, right_ref, down_ref, corner_ref, out_ref):
    side = tile_ref.shape[1]
    half = side // 2
    margin = down_ref.shape[1] // 2
    extra = margin - half
    largest = peak_ref[0]
    step = 8
    for row, packed, lane in pack_extra(side, extra, half):
        place = slice(row, row + step)
        for part in range(2):
            one = grad_ref[part, place, 0:half] + right_ref[part, place]
            two = grad_ref[part, place, half:side]
            piece = right_ref[part, side + packed : side + packed + 8, lane : lane + extra]
            if row < margin:
                one = one + down_ref[part, place] + corner_ref[part, place]
                two = two + down_ref[part, margin + row : margin + row + step]
                piece = piece + corner_ref[part, margin + packed : margin + packed + 8, lane : lane + extra]
            out_ref[part, place, 0:half] = tile_ref[part, place, 0:half] + one / largest
            out_ref[part, place, half:side] = tile_ref[part, place, half:side] + two / largest
            out_ref[part, place, half:margin] += piece / largest[:, 0:extra]


def body(object_field, probe_field, measured, positions):
    side = probe_field.shape[1]
    half = side // 2
    margin = HALO
    extra = margin - half
    frames = measured.shape[0]
    n_row, n_col = lax.axis_size("row"), lax.axis_size("col")
    fwd_right, fwd_left, inv_right, inv_left, lane_tw, row_tw = tables(side)
    wide = side + side * extra // half
    tall = margin + margin * extra // half

    near, far, right = pl.pallas_call(
        pack_kernel,
        out_shape=(f32(2, tall, half), f32(2, margin, half), f32(2, wide, half)),
        in_specs=[VMEM],
        out_specs=(VMEM,) * 3,
        cost_estimate=cost(10**6, 2 * 10**6),
        compiler_params=PARAMS,
    )(object_field)
    near = shifted(near, "row", -1)
    far = shifted(far, "row", -1)
    right = shifted(right, "col", -1)
    peak = pl.pallas_call(
        peak_kernel,
        out_shape=f32(2, 8, half),
        in_specs=[VMEM, VMEM],
        out_specs=VMEM,
        cost_estimate=cost(10**6, 2 * 10**6),
        compiler_params=PARAMS,
    )(probe_field, measured)
    near, peak = lax.optimization_barrier((near, peak))
    corner = shifted(near, "col", -1)
    places = positions.T
    prot, ampl = pl.pallas_call(
        prepare_kernel,
        out_shape=(f32(frames, 2, side, side), f32(frames, side, side)),
        in_specs=[SMEM, VMEM, VMEM],
        out_specs=(VMEM, VMEM),
        scratch_shapes=[pltpu.VMEM((2, 2, 2 * side, half), jnp.float32)],
        cost_estimate=cost(3 * 10**9, 6 * 10**6),
        compiler_params=PARAMS,
    )(places, probe_field, measured)
    depth = side // n_col
    g_tile, g_right, g_down, g_corner, sums = pl.pallas_call(
        frame_kernel,
        out_shape=(
            f32(2, side, side),
            f32(2, wide, half),
            f32(2, 2 * margin, half),
            f32(2, tall, half),
            f32(n_col, 3, depth, side),
        ),
        in_specs=[SMEM] + [VMEM] * 13,
        out_specs=(VMEM,) * 5,
        scratch_shapes=[
            pltpu.VMEM((2, side, half), jnp.float32),
            pltpu.VMEM((2, margin, half), jnp.float32),
            pltpu.VMEM((frames, 2, side, side), jnp.float32),
            pltpu.VMEM((2 * frames, side, 3 * side), BF16),
            pltpu.VMEM((2 * frames, 3 * side, side), BF16),
            pltpu.VMEM((2 * frames, side, side), jnp.float32),
            pltpu.VMEM((frames, 3, 2, side + margin, half), jnp.float32),
        ],
        cost_estimate=cost(6 * 10**9, 12 * 10**6),
        compiler_params=PARAMS,
    )(
        places, object_field, right, near, far, corner, prot, ampl,
        fwd_right, fwd_left, inv_right, inv_left, lane_tw, row_tw,
    )

    from_above = shifted(g_down, "row", 1)
    part = jnp.sum(lax.all_to_all(sums, "col", 0, 0), 0)
    part, from_above = lax.optimization_barrier((part, from_above))
    old = lax.dynamic_slice_in_dim(probe_field, lax.axis_index("col") * depth, depth, 1)
    terms = row_terms(part)
    g_right, terms[-1] = lax.optimization_barrier((g_right, terms[-1]))
    from_left = shifted(g_right, "col", 1)
    g_corner, terms[0] = lax.optimization_barrier((g_corner, terms[0]))
    from_corner = diagonal(g_corner)
    new = pl.pallas_call(
        update_kernel,
        out_shape=f32(n_col, 2, depth, side),
        in_specs=[VMEM] * (1 + len(terms)),
        out_specs=VMEM,
        cost_estimate=cost(10**6, 10**6),
        compiler_params=PARAMS,
    )(old, *terms)
    new = lax.all_to_all(new, "col", 0, 0)
    new_probe = new.transpose(1, 0, 2, 3).reshape(2, side, side)
    new_object = pl.pallas_call(
        finish_kernel,
        out_shape=f32(2, side, side),
        in_specs=[VMEM] * 6,
        out_specs=VMEM,
        cost_estimate=cost(10**6, 4 * 10**6),
        compiler_params=PARAMS,
    )(peak, object_field, g_tile, from_left, from_above, from_corner)
    return (new_object, new_probe)


def solution(mesh):
    in_specs = (P(None, "row", "col"), P(), P("row", "col", None), P("row", "col"))
    out_specs = (P(None, "row", "col"), P())
    return jax.shard_map(body, mesh=mesh, in_specs=in_specs, out_specs=out_specs, check_vma=False)
```

```python
import math

import jax
import jax.numpy as jnp
import numpy as np
from jax import lax
from jax.experimental import pallas as pl
from jax.experimental.pallas import tpu as pltpu
from jax.sharding import PartitionSpec as P

HALO = 160
VMEM = pl.BlockSpec(memory_space=pltpu.VMEM)
SMEM = pl.BlockSpec(memory_space=pltpu.SMEM)
PARAMS = pltpu.CompilerParams(vmem_limit_bytes=24 * 1024 * 1024)
BF16 = jnp.bfloat16


def shifted(value, axis, steps):
    count = lax.axis_size(axis)
    initial, last = (max(0, -steps), min(count, count - steps))
    return lax.ppermute(value, axis, [(source, source + steps) for source in range(initial, last)])


def diagonal(value):
    rows, cols = lax.axis_size("row"), lax.axis_size("col")
    pairs = [
        (row * cols + col, (row + 1) * cols + col + 1) for row in range(rows - 1) for col in range(cols - 1)
    ]
    return lax.ppermute(value, ("row", "col"), pairs)


def row_terms(value):
    rows = lax.axis_size("row")
    if rows != 4:
        return [lax.psum(value, "row")]
    three, two, one = (
        lax.ppermute(value, "row", [(row, row ^ step) for row in range(rows)]) for step in (3, 2, 1)
    )
    return [two, three, value, one]


def f32(*shape):
    return jax.ShapeDtypeStruct(shape, jnp.float32)


def cost(flops, moved):
    return pl.CostEstimate(flops=flops, bytes_accessed=moved, transcendentals=0)


def tables(side):
    half = side // 2
    index = np.arange(half)
    angle = 2.0 * math.pi / half * (np.outer(index, index) % half)
    cos = np.cos(angle) / math.sqrt(side)
    sin = -np.sin(angle) / math.sqrt(side)
    matrix = np.block([[cos, sin], [-sin, cos]])
    high = matrix.astype(BF16)
    low = (matrix - high.astype(np.float64)).astype(BF16)
    turn = -2.0 * math.pi / side * index
    twiddle = np.stack([np.cos(turn), np.sin(turn)]).astype(np.float32)
    lanes = np.ascontiguousarray(np.broadcast_to(twiddle[:, None, :], (2, 8, half)))
    rows = np.ascontiguousarray(np.broadcast_to(twiddle[:, :, None], (2, half, half)))
    return (
        np.concatenate([high, high, low], 0),
        np.concatenate([high.T, high.T, low.T], 1),
        np.concatenate([high.T, high.T, low.T], 0),
        np.concatenate([high, high, low], 1),
        lanes,
        rows,
    )


def dot(left, right):
    return jnp.dot(left, right, preferred_element_type=jnp.float32)


def halves(value):
    high = value.astype(BF16)
    low = (value - high.astype(jnp.float32)).astype(BF16)
    return high, low


def pack_extra(rows, extra, width):
    per = width // extra
    for group in range(rows // 8):
        yield group * 8, group // per * 8, group % per * extra


def pack_kernel(tile_ref, near_ref, far_ref, right_ref):
    side = tile_ref.shape[1]
    half = side // 2
    margin = far_ref.shape[1]
    extra = margin - half
    near_ref[:, 0:margin, :] = tile_ref[:, 0:margin, 0:half]
    far_ref[...] = tile_ref[:, 0:margin, half:]
    right_ref[:, 0:side, :] = tile_ref[:, :, 0:half]
    for row, packed, lane in pack_extra(side, extra, half):
        piece = tile_ref[:, row : row + 8, half:margin]
        right_ref[:, side + packed : side + packed + 8, lane : lane + extra] = piece
        if row < margin:
            near_ref[:, margin + packed : margin + packed + 8, lane : lane + extra] = piece


def peak_kernel(probe_ref, meas_ref, out_ref):
    re, im = probe_ref[0], probe_ref[1]
    top = jnp.max(re * re + im * im, axis=(0, 1), keepdims=True)
    out_ref[0] = jnp.broadcast_to(top, out_ref.shape[1:])
    out_ref[1] = meas_ref[0, 0:8, 0 : out_ref.shape[2]]


def turned(load, steps, half, lanes):
    within = lax.rem(steps, half)
    first = lax.rem(lax.div(steps, half), 2)
    back = lax.rem(half - within, half)
    one = pltpu.roll(load(first), back, 1)
    two = pltpu.roll(load(1 - first), back, 1)
    stay = lanes < half - within
    return jnp.where(stay, one, two), jnp.where(stay, two, one)


def prepare_kernel(pos_ref, probe_ref, meas_ref, prot_ref, sorted_ref, twice):
    frames, side = meas_ref.shape[0], meas_ref.shape[1]
    half = side // 2
    for part in range(2):
        for tile in range(2):
            piece = probe_ref[part, :, tile * half : (tile + 1) * half]
            twice[part, tile, 0:side] = piece
            twice[part, tile, side : 2 * side] = piece
    step = 64
    lanes = lax.broadcasted_iota(jnp.int32, (step, half), 1)
    rows = lax.broadcasted_iota(jnp.int32, (side, side), 0)
    cols = lax.broadcasted_iota(jnp.int32, (side, side), 1)
    sort = jnp.where(rows == jnp.where(cols < half, 2 * cols, 2 * cols - side + 1), 1.0, 0.0).astype(BF16)
    unsort = jnp.where(cols == jnp.where(rows < half, 2 * rows, 2 * rows - side + 1), 1.0, 0.0).astype(BF16)

    @pl.loop(0, frames)
    def _(frame):
        dy = pos_ref[0, frame]
        dx = pos_ref[1, frame]
        for part in range(2):
            for row in range(0, side, step):
                one, two = turned(
                    lambda tile: twice[part, tile, pl.ds(side - dy + row, step), :], side - dx, half, lanes
                )
                prot_ref[frame, part, row : row + step, 0:half] = one
                prot_ref[frame, part, row : row + step, half:side] = two
        value = meas_ref[frame]
        total = None
        for _ in range(3):
            piece = value.astype(BF16)
            value = value - piece.astype(jnp.float32)
            term = dot(dot(unsort, piece).astype(BF16), sort)
            total = term if total is None else total + term
        sorted_ref[frame] = total


def frame_kernel(
    pos_ref, tile_ref, right_ref, near_ref, far_ref, corner_ref, prot_ref, meas_ref,
    fwd_right, fwd_left, inv_right, inv_left, lane_ref, row_ref,
    gt_ref, gr_ref, gz_ref, gc_ref, qs_ref,
    right_extra, corner_extra, obj_ref, left_in, right_in, mid, twice,
):
    frames, side = meas_ref.shape[0], meas_ref.shape[1]
    half = side // 2
    margin = far_ref.shape[1]
    extra = margin - half
    for row, packed, lane in pack_extra(side, extra, half):
        right_extra[:, row : row + 8, 0:extra] = right_ref[:, side + packed : side + packed + 8, lane : lane + extra]
        if row < margin:
            corner_extra[:, row : row + 8, 0:extra] = corner_ref[
                :, margin + packed : margin + packed + 8, lane : lane + extra
            ]
    lane_cos, lane_sin = lane_ref[0, 0:1], lane_ref[1, 0:1]

    def store_left(where, rows, tile, value):
        high, low = halves(value)
        lane = tile * half
        where, rows = where // 2, slice(where % 2 * side + rows.start, where % 2 * side + rows.stop)
        left_in[where, rows, lane : lane + half] = high
        left_in[where, rows, side + lane : side + lane + half] = low
        left_in[where, rows, 2 * side + lane : 2 * side + lane + half] = high

    def store_right(where, row, count, columns, value):
        high, low = halves(value)
        right_in[where, row : row + count, columns] = high
        right_in[where, side + row : side + row + count, columns] = low
        right_in[where, 2 * side + row : 2 * side + row + count, columns] = high

    step = 32
    lanes = lax.broadcasted_iota(jnp.int32, (step, half), 1)
    row_in = lax.broadcasted_iota(jnp.int32, (step, half), 0)
    for frame in range(frames):
        dy = pos_ref[0, frame]
        dx = pos_ref[1, frame]
        own_col = (lanes >= dx, lanes + half >= dx)
        for row in range(0, side, step):
            rows = slice(row, row + step)
            own_row = row_in + row >= dy
            wave = []
            for tile in range(2):
                columns = slice(tile * half, (tile + 1) * half)
                obj = []
                for part in range(2):
                    right = right_extra[part, rows] if tile else right_ref[part, rows]
                    value = jnp.where(own_col[tile], tile_ref[part, rows, columns], right)
                    if row < margin:
                        below = far_ref[part, rows] if tile else near_ref[part, rows]
                        corner = corner_extra[part, rows] if tile else corner_ref[part, rows]
                        value = jnp.where(own_row, value, jnp.where(own_col[tile], below, corner))
                    obj_ref[frame, part, rows, columns] = value
                    obj.append(value)
                pro_re = prot_ref[frame, 0, rows, columns]
                pro_im = prot_ref[frame, 1, rows, columns]
                wave.append((pro_re * obj[0] - pro_im * obj[1], pro_re * obj[1] + pro_im * obj[0]))
            (re0, im0), (re1, im1) = wave
            store_left(2 * frame, rows, 0, re0 + re1)
            store_left(2 * frame, rows, 1, im0 + im1)
            re, im = re0 - re1, im0 - im1
            store_left(2 * frame + 1, rows, 0, re * lane_cos - im * lane_sin)
            store_left(2 * frame + 1, rows, 1, re * lane_sin + im * lane_cos)
        product = dot(left_in[frame], fwd_right[...])
        mid[2 * frame], mid[2 * frame + 1] = product[:side], product[side:]

    for frame in range(frames):
        for row in range(0, half, step):
            top, low = slice(row, row + step), slice(half + row, half + row + step)
            row_cos, row_sin = row_ref[0, top], row_ref[1, top]
            for which in range(2):
                columns = slice(which * half, (which + 1) * half)
                top_re, top_im = mid[2 * frame + which, top, 0:half], mid[2 * frame + which, top, half:side]
                low_re, low_im = mid[2 * frame + which, low, 0:half], mid[2 * frame + which, low, half:side]
                store_right(2 * frame, row, step, columns, top_re + low_re)
                store_right(2 * frame, half + row, step, columns, top_im + low_im)
                re, im = top_re - low_re, top_im - low_im
                store_right(2 * frame + 1, row, step, columns, re * row_cos - im * row_sin)
                store_right(2 * frame + 1, half + row, step, columns, re * row_sin + im * row_cos)
        for which in range(2):
            mid[2 * frame + which] = dot(fwd_left[...], right_in[2 * frame + which])

    for frame in range(frames):
        for which in range(2):
            for row in range(0, half, step):
                re = mid[2 * frame + which, row : row + step]
                im = mid[2 * frame + which, half + row : half + row + step]
                ampl = meas_ref[frame, which * half + row : which * half + row + step]
                factor = ampl * lax.rsqrt(jnp.maximum(re * re + im * im, 0.25)) - 1.0
                store_right(2 * frame + which, row, step, slice(0, side), factor * re)
                store_right(2 * frame + which, half + row, step, slice(0, side), factor * im)
            mid[2 * frame + which] = dot(inv_left[...], right_in[2 * frame + which])

    for frame in range(frames):
        for row in range(0, half, step):
            top, low = slice(row, row + step), slice(half + row, half + row + step)
            row_cos, row_sin = row_ref[0, top], row_ref[1, top]
            for which in range(2):
                columns = slice(which * half, (which + 1) * half)
                even_re, even_im = mid[2 * frame, top, columns], mid[2 * frame, low, columns]
                odd_re, odd_im = mid[2 * frame + 1, top, columns], mid[2 * frame + 1, low, columns]
                re = odd_re * row_cos + odd_im * row_sin
                im = odd_im * row_cos - odd_re * row_sin
                store_left(2 * frame + which, top, 0, even_re + re)
                store_left(2 * frame + which, top, 1, even_im + im)
                store_left(2 * frame + which, low, 0, even_re - re)
                store_left(2 * frame + which, low, 1, even_im - im)
        product = dot(left_in[frame], inv_right[...])
        mid[2 * frame], mid[2 * frame + 1] = product[:side], product[side:]

    step = 8
    lanes = lax.broadcasted_iota(jnp.int32, (step, half), 1)
    row_in = lax.broadcasted_iota(jnp.int32, (step, half), 0)
    places = {row: (packed, lane) for row, packed, lane in pack_extra(side, extra, half)}
    for row in range(0, side, step):
        rows = slice(row, row + step)
        total = {}
        for frame in range(frames):
            dy = pos_ref[0, frame]
            dx = pos_ref[1, frame]
            masks = []
            for tile in range(2):
                own_col = lanes + tile * half >= dx
                far_col = jnp.logical_not(own_col)
                if row < margin:
                    own_row = row_in + row >= dy
                    far_row = jnp.logical_not(own_row)
                    masks.append(
                        {"t": own_row & own_col, "r": own_row & far_col, "b": far_row & own_col, "c": far_row & far_col}
                    )
                else:
                    masks.append({"t": own_col, "r": far_col})
            even_re, even_im = mid[2 * frame, rows, 0:half], mid[2 * frame, rows, half:side]
            odd_re, odd_im = mid[2 * frame + 1, rows, 0:half], mid[2 * frame + 1, rows, half:side]
            re = odd_re * lane_cos + odd_im * lane_sin
            im = odd_im * lane_cos - odd_re * lane_sin
            for tile in range(2):
                columns = slice(tile * half, (tile + 1) * half)
                chi_re = even_re - re if tile else even_re + re
                chi_im = even_im - im if tile else even_im + im
                pro_re = prot_ref[frame, 0, rows, columns]
                pro_im = prot_ref[frame, 1, rows, columns]
                obj_re = obj_ref[frame, 0, rows, columns]
                obj_im = obj_ref[frame, 1, rows, columns]
                for part, value in enumerate(
                    (pro_re * chi_re + pro_im * chi_im, pro_re * chi_im - pro_im * chi_re)
                ):
                    for name, mask in masks[tile].items():
                        piece = jnp.where(mask, value, 0.0)
                        key = (name, part, tile)
                        total[key] = piece if frame == 0 else total[key] + piece
                for index, value in enumerate(
                    (
                        obj_re * chi_re + obj_im * chi_im,
                        obj_re * chi_im - obj_im * chi_re,
                        obj_re * obj_re + obj_im * obj_im,
                    )
                ):
                    twice[frame, index, tile, row : row + step] = value
                    if row < margin:
                        twice[frame, index, tile, side + row : side + row + step] = value
        packed, lane = places[row]
        for part in range(2):
            gt_ref[part, rows, 0:half] = total["t", part, 0]
            gt_ref[part, rows, half:side] = total["t", part, 1]
            gr_ref[part, rows] = total["r", part, 0]
            gr_ref[part, side + packed : side + packed + 8, lane : lane + extra] = total["r", part, 1][:, 0:extra]
            if row < margin:
                gz_ref[part, rows] = total["b", part, 0]
                gz_ref[part, margin + row : margin + row + step] = total["b", part, 1]
                gc_ref[part, rows] = total["c", part, 0]
                base = margin + packed
                gc_ref[part, base : base + 8, lane : lane + extra] = total["c", part, 1][:, 0:extra]

    depth = qs_ref.shape[2]
    step = min(32, depth)
    lanes = lax.broadcasted_iota(jnp.int32, (step, half), 1)
    for row in range(0, side, step):
        for index in range(3):
            sums = None
            for frame in range(frames):
                dy = pos_ref[0, frame]
                dx = pos_ref[1, frame]
                pair = turned(
                    lambda tile: twice[frame, index, tile, pl.ds(dy + row, step), :], dx, half, lanes
                )
                sums = pair if sums is None else (sums[0] + pair[0], sums[1] + pair[1])
            place = slice(row % depth, row % depth + step)
            qs_ref[row // depth, index, place, 0:half] = sums[0]
            qs_ref[row // depth, index, place, half:side] = sums[1]


def update_kernel(old_ref, *refs):
    terms, out_ref = refs[:-1], refs[-1]

    def total(index):
        values = [term[index] for term in terms]
        while len(values) > 1:
            values = [values[at] + values[at + 1] for at in range(0, len(values), 2)]
        return values[0]

    weight = total(2) + 1.0
    for part in range(2):
        value = old_ref[part] + total(part) / weight
        for copy in range(out_ref.shape[0]):
            out_ref[copy, part] = value


def finish_kernel(peak_ref, tile_ref, grad_ref, right_ref, down_ref, corner_ref, new_ref, out_ref, probe_ref):
    side = tile_ref.shape[1]
    half = side // 2
    margin = down_ref.shape[1] // 2
    extra = margin - half
    depth = new_ref.shape[2]
    for block in range(new_ref.shape[0]):
        probe_ref[:, block * depth : (block + 1) * depth, :] = new_ref[block]
    largest = peak_ref[0]
    step = 8
    for row, packed, lane in pack_extra(side, extra, half):
        place = slice(row, row + step)
        for part in range(2):
            one = grad_ref[part, place, 0:half] + right_ref[part, place]
            two = grad_ref[part, place, half:side]
            piece = right_ref[part, side + packed : side + packed + 8, lane : lane + extra]
            if row < margin:
                one = one + down_ref[part, place] + corner_ref[part, place]
                two = two + down_ref[part, margin + row : margin + row + step]
                piece = piece + corner_ref[part, margin + packed : margin + packed + 8, lane : lane + extra]
            out_ref[part, place, 0:half] = tile_ref[part, place, 0:half] + one / largest
            out_ref[part, place, half:side] = tile_ref[part, place, half:side] + two / largest
            out_ref[part, place, half:margin] += piece / largest[:, 0:extra]


def body(object_field, probe_field, measured, positions):
    side = probe_field.shape[1]
    half = side // 2
    margin = HALO
    extra = margin - half
    frames = measured.shape[0]
    n_row, n_col = lax.axis_size("row"), lax.axis_size("col")
    fwd_right, fwd_left, inv_right, inv_left, lane_tw, row_tw = tables(side)
    wide = side + side * extra // half
    tall = margin + margin * extra // half

    near, far, right = pl.pallas_call(
        pack_kernel,
        out_shape=(f32(2, tall, half), f32(2, margin, half), f32(2, wide, half)),
        in_specs=[VMEM],
        out_specs=(VMEM,) * 3,
        cost_estimate=cost(10**6, 2 * 10**6),
        compiler_params=PARAMS,
    )(object_field)
    near = shifted(near, "row", -1)
    far = shifted(far, "row", -1)
    right = shifted(right, "col", -1)
    peak = pl.pallas_call(
        peak_kernel,
        out_shape=f32(2, 8, half),
        in_specs=[VMEM, VMEM],
        out_specs=VMEM,
        cost_estimate=cost(10**6, 2 * 10**6),
        compiler_params=PARAMS,
    )(probe_field, measured)
    near, peak = lax.optimization_barrier((near, peak))
    corner = shifted(near, "col", -1)
    places = positions.T
    prot, ampl = pl.pallas_call(
        prepare_kernel,
        out_shape=(f32(frames, 2, side, side), f32(frames, side, side)),
        in_specs=[SMEM, VMEM, VMEM],
        out_specs=(VMEM, VMEM),
        scratch_shapes=[pltpu.VMEM((2, 2, 2 * side, half), jnp.float32)],
        cost_estimate=cost(3 * 10**9, 6 * 10**6),
        compiler_params=PARAMS,
    )(places, probe_field, measured)
    depth = side // n_col
    g_tile, g_right, g_down, g_corner, sums = pl.pallas_call(
        frame_kernel,
        out_shape=(
            f32(2, side, side),
            f32(2, wide, half),
            f32(2, 2 * margin, half),
            f32(2, tall, half),
            f32(n_col, 3, depth, side),
        ),
        in_specs=[SMEM] + [VMEM] * 13,
        out_specs=(VMEM,) * 5,
        scratch_shapes=[
            pltpu.VMEM((2, side, half), jnp.float32),
            pltpu.VMEM((2, margin, half), jnp.float32),
            pltpu.VMEM((frames, 2, side, side), jnp.float32),
            pltpu.VMEM((frames, 2 * side, 3 * side), BF16),
            pltpu.VMEM((2 * frames, 3 * side, side), BF16),
            pltpu.VMEM((2 * frames, side, side), jnp.float32),
            pltpu.VMEM((frames, 3, 2, side + margin, half), jnp.float32),
        ],
        cost_estimate=cost(6 * 10**9, 12 * 10**6),
        compiler_params=PARAMS,
    )(
        places, object_field, right, near, far, corner, prot, ampl,
        fwd_right, fwd_left, inv_right, inv_left, lane_tw, row_tw,
    )

    from_above = shifted(g_down, "row", 1)
    part = jnp.sum(lax.all_to_all(sums, "col", 0, 0), 0)
    part, from_above, g_right = lax.optimization_barrier((part, from_above, g_right))
    old = lax.dynamic_slice_in_dim(probe_field, lax.axis_index("col") * depth, depth, 1)
    terms = row_terms(part)
    from_left = shifted(g_right, "col", 1)
    g_corner, terms[0] = lax.optimization_barrier((g_corner, terms[0]))
    from_corner = diagonal(g_corner)
    new = pl.pallas_call(
        update_kernel,
        out_shape=f32(n_col, 2, depth, side),
        in_specs=[VMEM] * (1 + len(terms)),
        out_specs=VMEM,
        cost_estimate=cost(10**10, 10**6),
        compiler_params=PARAMS,
    )(old, *terms)
    new, from_left = lax.optimization_barrier((new, from_left))
    new = lax.all_to_all(new, "col", 0, 0)
    new_object, new_probe = pl.pallas_call(
        finish_kernel,
        out_shape=(f32(2, side, side), f32(2, side, side)),
        in_specs=[VMEM] * 7,
        out_specs=(VMEM, VMEM),
        cost_estimate=cost(10**6, 4 * 10**6),
        compiler_params=PARAMS,
    )(peak, object_field, g_tile, from_left, from_above, from_corner, new)
    return (new_object, new_probe)


def solution(mesh):
    in_specs = (P(None, "row", "col"), P(), P("row", "col", None), P("row", "col"))
    out_specs = (P(None, "row", "col"), P())
    return jax.shard_map(body, mesh=mesh, in_specs=in_specs, out_specs=out_specs, check_vma=False)
```

```python
import math

import jax
import jax.numpy as jnp
import numpy as np
from jax import lax
from jax.experimental import pallas as pl
from jax.experimental.pallas import tpu as pltpu
from jax.sharding import PartitionSpec as P

HALO = 160
VMEM = pl.BlockSpec(memory_space=pltpu.VMEM)
SMEM = pl.BlockSpec(memory_space=pltpu.SMEM)
PARAMS = pltpu.CompilerParams(vmem_limit_bytes=24 * 1024 * 1024)
BF16 = jnp.bfloat16


def shifted(value, axis, steps):
    count = lax.axis_size(axis)
    initial, last = (max(0, -steps), min(count, count - steps))
    return lax.ppermute(value, axis, [(source, source + steps) for source in range(initial, last)])


def diagonal(value):
    rows, cols = lax.axis_size("row"), lax.axis_size("col")
    pairs = [
        (row * cols + col, (row + 1) * cols + col + 1) for row in range(rows - 1) for col in range(cols - 1)
    ]
    return lax.ppermute(value, ("row", "col"), pairs)


def row_terms(value):
    rows = lax.axis_size("row")
    if rows != 4:
        return [lax.psum(value, "row")]
    three, two, one = (
        lax.ppermute(value, "row", [(row, row ^ step) for row in range(rows)]) for step in (3, 2, 1)
    )
    return [two, three, value, one]


def f32(*shape):
    return jax.ShapeDtypeStruct(shape, jnp.float32)


def cost(flops, moved):
    return pl.CostEstimate(flops=flops, bytes_accessed=moved, transcendentals=0)


def tables(side):
    half = side // 2
    index = np.arange(half)
    angle = 2.0 * math.pi / half * (np.outer(index, index) % half)
    cos = np.cos(angle) / math.sqrt(side)
    sin = -np.sin(angle) / math.sqrt(side)
    matrix = np.block([[cos, sin], [-sin, cos]])
    high = matrix.astype(BF16)
    low = (matrix - high.astype(np.float64)).astype(BF16)
    turn = -2.0 * math.pi / side * index
    twiddle = np.stack([np.cos(turn), np.sin(turn)]).astype(np.float32)
    lanes = np.ascontiguousarray(np.broadcast_to(twiddle[:, None, :], (2, 8, half)))
    rows = np.ascontiguousarray(np.broadcast_to(twiddle[:, :, None], (2, half, half)))
    return (
        np.concatenate([high, high, low], 0),
        np.concatenate([high.T, high.T, low.T], 1),
        np.concatenate([high.T, high.T, low.T], 0),
        np.concatenate([high, high, low], 1),
        lanes,
        rows,
    )


def dot(left, right):
    return jnp.dot(left, right, preferred_element_type=jnp.float32)


def halves(value):
    high = value.astype(BF16)
    low = (value - high.astype(jnp.float32)).astype(BF16)
    return high, low


def pack_extra(rows, extra, width):
    per = width // extra
    for group in range(rows // 8):
        yield group * 8, group // per * 8, group % per * extra


def pack_kernel(tile_ref, near_ref, far_ref, right_ref):
    side = tile_ref.shape[1]
    half = side // 2
    margin = far_ref.shape[1]
    extra = margin - half
    near_ref[:, 0:margin, :] = tile_ref[:, 0:margin, 0:half]
    far_ref[...] = tile_ref[:, 0:margin, half:]
    right_ref[:, 0:side, :] = tile_ref[:, :, 0:half]
    for row, packed, lane in pack_extra(side, extra, half):
        piece = tile_ref[:, row : row + 8, half:margin]
        right_ref[:, side + packed : side + packed + 8, lane : lane + extra] = piece
        if row < margin:
            near_ref[:, margin + packed : margin + packed + 8, lane : lane + extra] = piece


def peak_kernel(probe_ref, meas_ref, out_ref):
    re, im = probe_ref[0], probe_ref[1]
    top = jnp.max(re * re + im * im, axis=(0, 1), keepdims=True)
    out_ref[0] = jnp.broadcast_to(top, out_ref.shape[1:])
    out_ref[1] = meas_ref[0, 0:8, 0 : out_ref.shape[2]]


def turned(load, steps, half, lanes):
    within = lax.rem(steps, half)
    first = lax.rem(lax.div(steps, half), 2)
    back = lax.rem(half - within, half)
    one = pltpu.roll(load(first), back, 1)
    two = pltpu.roll(load(1 - first), back, 1)
    stay = lanes < half - within
    return jnp.where(stay, one, two), jnp.where(stay, two, one)


def prepare_kernel(pos_ref, probe_ref, meas_ref, prot_ref, sorted_ref, twice):
    frames, side = meas_ref.shape[0], meas_ref.shape[1]
    half = side // 2
    for part in range(2):
        for tile in range(2):
            piece = probe_ref[part, :, tile * half : (tile + 1) * half]
            twice[part, tile, 0:side] = piece
            twice[part, tile, side : 2 * side] = piece
    step = 64
    lanes = lax.broadcasted_iota(jnp.int32, (step, half), 1)
    rows = lax.broadcasted_iota(jnp.int32, (side, side), 0)
    cols = lax.broadcasted_iota(jnp.int32, (side, side), 1)
    sort = jnp.where(rows == jnp.where(cols < half, 2 * cols, 2 * cols - side + 1), 1.0, 0.0).astype(BF16)
    unsort = jnp.where(cols == jnp.where(rows < half, 2 * rows, 2 * rows - side + 1), 1.0, 0.0).astype(BF16)

    @pl.loop(0, frames)
    def _(frame):
        dy = pos_ref[0, frame]
        dx = pos_ref[1, frame]
        for part in range(2):
            for row in range(0, side, step):
                one, two = turned(
                    lambda tile: twice[part, tile, pl.ds(side - dy + row, step), :], side - dx, half, lanes
                )
                prot_ref[frame, part, row : row + step, 0:half] = one
                prot_ref[frame, part, row : row + step, half:side] = two
        value = meas_ref[frame]
        total = None
        for _ in range(3):
            piece = value.astype(BF16)
            value = value - piece.astype(jnp.float32)
            term = dot(dot(unsort, piece).astype(BF16), sort)
            total = term if total is None else total + term
        sorted_ref[frame] = total


def frame_kernel(
    pos_ref, tile_ref, right_ref, near_ref, far_ref, corner_ref, prot_ref, meas_ref,
    fwd_right, fwd_left, inv_right, inv_left, lane_ref, row_ref,
    gt_ref, gr_ref, gz_ref, gc_ref, qs_ref,
    right_extra, corner_extra, obj_ref, left_in, right_in, mid, twice,
):
    frames, side = meas_ref.shape[0], meas_ref.shape[1]
    half = side // 2
    margin = far_ref.shape[1]
    extra = margin - half
    for row, packed, lane in pack_extra(side, extra, half):
        right_extra[:, row : row + 8, 0:extra] = right_ref[:, side + packed : side + packed + 8, lane : lane + extra]
        if row < margin:
            corner_extra[:, row : row + 8, 0:extra] = corner_ref[
                :, margin + packed : margin + packed + 8, lane : lane + extra
            ]
    lane_cos, lane_sin = lane_ref[0, 0:1], lane_ref[1, 0:1]

    def store_left(where, rows, tile, value):
        high, low = halves(value)
        lane = tile * half
        left_in[where, rows, lane : lane + half] = high
        left_in[where, rows, side + lane : side + lane + half] = low
        left_in[where, rows, 2 * side + lane : 2 * side + lane + half] = high

    def store_right(where, row, count, columns, value):
        high, low = halves(value)
        right_in[where, row : row + count, columns] = high
        right_in[where, side + row : side + row + count, columns] = low
        right_in[where, 2 * side + row : 2 * side + row + count, columns] = high

    step = 32
    lanes = lax.broadcasted_iota(jnp.int32, (step, half), 1)
    row_in = lax.broadcasted_iota(jnp.int32, (step, half), 0)
    for frame in range(frames):
        dy = pos_ref[0, frame]
        dx = pos_ref[1, frame]
        own_col = (lanes >= dx, lanes + half >= dx)
        for row in range(0, side, step):
            rows = slice(row, row + step)
            own_row = row_in + row >= dy
            wave = []
            for tile in range(2):
                columns = slice(tile * half, (tile + 1) * half)
                obj = []
                for part in range(2):
                    right = right_extra[part, rows] if tile else right_ref[part, rows]
                    value = jnp.where(own_col[tile], tile_ref[part, rows, columns], right)
                    if row < margin:
                        below = far_ref[part, rows] if tile else near_ref[part, rows]
                        corner = corner_extra[part, rows] if tile else corner_ref[part, rows]
                        value = jnp.where(own_row, value, jnp.where(own_col[tile], below, corner))
                    obj_ref[frame, part, rows, columns] = value
                    obj.append(value)
                pro_re = prot_ref[frame, 0, rows, columns]
                pro_im = prot_ref[frame, 1, rows, columns]
                wave.append((pro_re * obj[0] - pro_im * obj[1], pro_re * obj[1] + pro_im * obj[0]))
            (re0, im0), (re1, im1) = wave
            store_left(2 * frame, rows, 0, re0 + re1)
            store_left(2 * frame, rows, 1, im0 + im1)
            re, im = re0 - re1, im0 - im1
            store_left(2 * frame + 1, rows, 0, re * lane_cos - im * lane_sin)
            store_left(2 * frame + 1, rows, 1, re * lane_sin + im * lane_cos)
        for which in range(2):
            mid[2 * frame + which] = dot(left_in[2 * frame + which], fwd_right[...])

    for frame in range(frames):
        for row in range(0, half, step):
            top, low = slice(row, row + step), slice(half + row, half + row + step)
            row_cos, row_sin = row_ref[0, top], row_ref[1, top]
            for which in range(2):
                columns = slice(which * half, (which + 1) * half)
                top_re, top_im = mid[2 * frame + which, top, 0:half], mid[2 * frame + which, top, half:side]
                low_re, low_im = mid[2 * frame + which, low, 0:half], mid[2 * frame + which, low, half:side]
                store_right(2 * frame, row, step, columns, top_re + low_re)
                store_right(2 * frame, half + row, step, columns, top_im + low_im)
                re, im = top_re - low_re, top_im - low_im
                store_right(2 * frame + 1, row, step, columns, re * row_cos - im * row_sin)
                store_right(2 * frame + 1, half + row, step, columns, re * row_sin + im * row_cos)
        for which in range(2):
            mid[2 * frame + which] = dot(fwd_left[...], right_in[2 * frame + which])

    for frame in range(frames):
        for which in range(2):
            for row in range(0, half, step):
                re = mid[2 * frame + which, row : row + step]
                im = mid[2 * frame + which, half + row : half + row + step]
                ampl = meas_ref[frame, which * half + row : which * half + row + step]
                factor = ampl * lax.rsqrt(jnp.maximum(re * re + im * im, 0.25)) - 1.0
                store_right(2 * frame + which, row, step, slice(0, side), factor * re)
                store_right(2 * frame + which, half + row, step, slice(0, side), factor * im)
            mid[2 * frame + which] = dot(inv_left[...], right_in[2 * frame + which])

    for frame in range(frames):
        for row in range(0, half, step):
            top, low = slice(row, row + step), slice(half + row, half + row + step)
            row_cos, row_sin = row_ref[0, top], row_ref[1, top]
            for which in range(2):
                columns = slice(which * half, (which + 1) * half)
                even_re, even_im = mid[2 * frame, top, columns], mid[2 * frame, low, columns]
                odd_re, odd_im = mid[2 * frame + 1, top, columns], mid[2 * frame + 1, low, columns]
                re = odd_re * row_cos + odd_im * row_sin
                im = odd_im * row_cos - odd_re * row_sin
                store_left(2 * frame + which, top, 0, even_re + re)
                store_left(2 * frame + which, top, 1, even_im + im)
                store_left(2 * frame + which, low, 0, even_re - re)
                store_left(2 * frame + which, low, 1, even_im - im)
        for which in range(2):
            mid[2 * frame + which] = dot(left_in[2 * frame + which], inv_right[...])

    step = 8
    lanes = lax.broadcasted_iota(jnp.int32, (step, half), 1)
    row_in = lax.broadcasted_iota(jnp.int32, (step, half), 0)
    places = {row: (packed, lane) for row, packed, lane in pack_extra(side, extra, half)}
    for row in range(0, side, step):
        rows = slice(row, row + step)
        total = {}
        for frame in range(frames):
            dy = pos_ref[0, frame]
            dx = pos_ref[1, frame]
            masks = []
            for tile in range(2):
                own_col = lanes + tile * half >= dx
                far_col = jnp.logical_not(own_col)
                if row < margin:
                    own_row = row_in + row >= dy
                    far_row = jnp.logical_not(own_row)
                    masks.append(
                        {"t": own_row & own_col, "r": own_row & far_col, "b": far_row & own_col, "c": far_row & far_col}
                    )
                else:
                    masks.append({"t": own_col, "r": far_col})
            even_re, even_im = mid[2 * frame, rows, 0:half], mid[2 * frame, rows, half:side]
            odd_re, odd_im = mid[2 * frame + 1, rows, 0:half], mid[2 * frame + 1, rows, half:side]
            re = odd_re * lane_cos + odd_im * lane_sin
            im = odd_im * lane_cos - odd_re * lane_sin
            for tile in range(2):
                columns = slice(tile * half, (tile + 1) * half)
                chi_re = even_re - re if tile else even_re + re
                chi_im = even_im - im if tile else even_im + im
                pro_re = prot_ref[frame, 0, rows, columns]
                pro_im = prot_ref[frame, 1, rows, columns]
                obj_re = obj_ref[frame, 0, rows, columns]
                obj_im = obj_ref[frame, 1, rows, columns]
                for part, value in enumerate(
                    (pro_re * chi_re + pro_im * chi_im, pro_re * chi_im - pro_im * chi_re)
                ):
                    for name, mask in masks[tile].items():
                        piece = jnp.where(mask, value, 0.0)
                        key = (name, part, tile)
                        total[key] = piece if frame == 0 else total[key] + piece
                for index, value in enumerate(
                    (
                        obj_re * chi_re + obj_im * chi_im,
                        obj_re * chi_im - obj_im * chi_re,
                        obj_re * obj_re + obj_im * obj_im,
                    )
                ):
                    twice[frame, index, tile, row : row + step] = value
                    if row < margin:
                        twice[frame, index, tile, side + row : side + row + step] = value
        packed, lane = places[row]
        for part in range(2):
            gt_ref[part, rows, 0:half] = total["t", part, 0]
            gt_ref[part, rows, half:side] = total["t", part, 1]
            gr_ref[part, rows] = total["r", part, 0]
            gr_ref[part, side + packed : side + packed + 8, lane : lane + extra] = total["r", part, 1][:, 0:extra]
            if row < margin:
                gz_ref[part, rows] = total["b", part, 0]
                gz_ref[part, margin + row : margin + row + step] = total["b", part, 1]
                gc_ref[part, rows] = total["c", part, 0]
                base = margin + packed
                gc_ref[part, base : base + 8, lane : lane + extra] = total["c", part, 1][:, 0:extra]

    depth = qs_ref.shape[2]
    step = min(32, depth)
    lanes = lax.broadcasted_iota(jnp.int32, (step, half), 1)
    for row in range(0, side, step):
        for index in range(3):
            sums = None
            for frame in range(frames):
                dy = pos_ref[0, frame]
                dx = pos_ref[1, frame]
                pair = turned(
                    lambda tile: twice[frame, index, tile, pl.ds(dy + row, step), :], dx, half, lanes
                )
                sums = pair if sums is None else (sums[0] + pair[0], sums[1] + pair[1])
            place = slice(row % depth, row % depth + step)
            qs_ref[row // depth, index, place, 0:half] = sums[0]
            qs_ref[row // depth, index, place, half:side] = sums[1]


def update_kernel(old_ref, *refs):
    terms, out_ref = refs[:-1], refs[-1]

    def total(index):
        values = [term[index] for term in terms]
        while len(values) > 1:
            values = [values[at] + values[at + 1] for at in range(0, len(values), 2)]
        return values[0]

    weight = total(2) + 1.0
    for part in range(2):
        value = old_ref[part] + total(part) / weight
        for copy in range(out_ref.shape[0]):
            out_ref[copy, part] = value


def finish_kernel(peak_ref, tile_ref, grad_ref, right_ref, down_ref, corner_ref, new_ref, out_ref, probe_ref):
    side = tile_ref.shape[1]
    half = side // 2
    margin = down_ref.shape[1] // 2
    extra = margin - half
    depth = new_ref.shape[2]
    for block in range(new_ref.shape[0]):
        probe_ref[:, block * depth : (block + 1) * depth, :] = new_ref[block]
    largest = peak_ref[0]
    step = 8
    for row, packed, lane in pack_extra(side, extra, half):
        place = slice(row, row + step)
        for part in range(2):
            one = grad_ref[part, place, 0:half] + right_ref[part, place]
            two = grad_ref[part, place, half:side]
            piece = right_ref[part, side + packed : side + packed + 8, lane : lane + extra]
            if row < margin:
                one = one + down_ref[part, place] + corner_ref[part, place]
                two = two + down_ref[part, margin + row : margin + row + step]
                piece = piece + corner_ref[part, margin + packed : margin + packed + 8, lane : lane + extra]
            out_ref[part, place, 0:half] = tile_ref[part, place, 0:half] + one / largest
            out_ref[part, place, half:side] = tile_ref[part, place, half:side] + two / largest
            out_ref[part, place, half:margin] += piece / largest[:, 0:extra]


def body(object_field, probe_field, measured, positions):
    side = probe_field.shape[1]
    half = side // 2
    margin = HALO
    extra = margin - half
    frames = measured.shape[0]
    n_row, n_col = lax.axis_size("row"), lax.axis_size("col")
    fwd_right, fwd_left, inv_right, inv_left, lane_tw, row_tw = tables(side)
    wide = side + side * extra // half
    tall = margin + margin * extra // half

    near, far, right = pl.pallas_call(
        pack_kernel,
        out_shape=(f32(2, tall, half), f32(2, margin, half), f32(2, wide, half)),
        in_specs=[VMEM],
        out_specs=(VMEM,) * 3,
        cost_estimate=cost(10**6, 2 * 10**6),
        compiler_params=PARAMS,
    )(object_field)
    near = shifted(near, "row", -1)
    far = shifted(far, "row", -1)
    right = shifted(right, "col", -1)
    near, probe, ampl = lax.optimization_barrier((near, probe_field, measured))
    peak = pl.pallas_call(
        peak_kernel,
        out_shape=f32(2, 8, half),
        in_specs=[VMEM, VMEM],
        out_specs=VMEM,
        cost_estimate=cost(10**6, 2 * 10**6),
        compiler_params=PARAMS,
    )(probe, ampl)
    corner = shifted(near, "col", -1)
    places = positions.T
    prot, ampl = pl.pallas_call(
        prepare_kernel,
        out_shape=(f32(frames, 2, side, side), f32(frames, side, side)),
        in_specs=[SMEM, VMEM, VMEM],
        out_specs=(VMEM, VMEM),
        scratch_shapes=[pltpu.VMEM((2, 2, 2 * side, half), jnp.float32)],
        cost_estimate=cost(3 * 10**9, 6 * 10**6),
        compiler_params=PARAMS,
    )(places, probe, ampl)
    depth = side // n_col
    g_tile, g_right, g_down, g_corner, sums = pl.pallas_call(
        frame_kernel,
        out_shape=(
            f32(2, side, side),
            f32(2, wide, half),
            f32(2, 2 * margin, half),
            f32(2, tall, half),
            f32(n_col, 3, depth, side),
        ),
        in_specs=[SMEM] + [VMEM] * 13,
        out_specs=(VMEM,) * 5,
        scratch_shapes=[
            pltpu.VMEM((2, side, half), jnp.float32),
            pltpu.VMEM((2, margin, half), jnp.float32),
            pltpu.VMEM((frames, 2, side, side), jnp.float32),
            pltpu.VMEM((2 * frames, side, 3 * side), BF16),
            pltpu.VMEM((2 * frames, 3 * side, side), BF16),
            pltpu.VMEM((2 * frames, side, side), jnp.float32),
            pltpu.VMEM((frames, 3, 2, side + margin, half), jnp.float32),
        ],
        cost_estimate=cost(6 * 10**9, 12 * 10**6),
        compiler_params=PARAMS,
    )(
        places, object_field, right, near, far, corner, prot, ampl,
        fwd_right, fwd_left, inv_right, inv_left, lane_tw, row_tw,
    )

    from_above = shifted(g_down, "row", 1)
    part = jnp.sum(lax.all_to_all(sums, "col", 0, 0), 0)
    part, from_above, g_right = lax.optimization_barrier((part, from_above, g_right))
    old = lax.dynamic_slice_in_dim(probe_field, lax.axis_index("col") * depth, depth, 1)
    terms = row_terms(part)
    from_left = shifted(g_right, "col", 1)
    g_corner, terms[0] = lax.optimization_barrier((g_corner, terms[0]))
    from_corner = diagonal(g_corner)
    new = pl.pallas_call(
        update_kernel,
        out_shape=f32(n_col, 2, depth, side),
        in_specs=[VMEM] * (1 + len(terms)),
        out_specs=VMEM,
        cost_estimate=cost(10**10, 10**6),
        compiler_params=PARAMS,
    )(old, *terms)
    new, from_left = lax.optimization_barrier((new, from_left))
    new = lax.all_to_all(new, "col", 0, 0)
    new_object, new_probe = pl.pallas_call(
        finish_kernel,
        out_shape=(f32(2, side, side), f32(2, side, side)),
        in_specs=[VMEM] * 7,
        out_specs=(VMEM, VMEM),
        cost_estimate=cost(10**6, 4 * 10**6),
        compiler_params=PARAMS,
    )(peak, object_field, g_tile, from_left, from_above, from_corner, new)
    return (new_object, new_probe)


def solution(mesh):
    in_specs = (P(None, "row", "col"), P(), P("row", "col", None), P("row", "col"))
    out_specs = (P(None, "row", "col"), P())
    return jax.shard_map(body, mesh=mesh, in_specs=in_specs, out_specs=out_specs, check_vma=False)
```

```python
import math

import jax
import jax.numpy as jnp
import numpy as np
from jax import lax
from jax.experimental import pallas as pl
from jax.experimental.pallas import tpu as pltpu
from jax.sharding import PartitionSpec as P

HALO = 160
VMEM = pl.BlockSpec(memory_space=pltpu.VMEM)
SMEM = pl.BlockSpec(memory_space=pltpu.SMEM)
PARAMS = pltpu.CompilerParams(vmem_limit_bytes=24 * 1024 * 1024)
BF16 = jnp.bfloat16


def shifted(value, axis, steps):
    count = lax.axis_size(axis)
    initial, last = (max(0, -steps), min(count, count - steps))
    return lax.ppermute(value, axis, [(source, source + steps) for source in range(initial, last)])


def diagonal(value):
    rows, cols = lax.axis_size("row"), lax.axis_size("col")
    pairs = [
        (row * cols + col, (row + 1) * cols + col + 1) for row in range(rows - 1) for col in range(cols - 1)
    ]
    return lax.ppermute(value, ("row", "col"), pairs)


def row_terms(value):
    rows = lax.axis_size("row")
    if rows != 4:
        return [lax.psum(value, "row")]
    three, two, one = (
        lax.ppermute(value, "row", [(row, row ^ step) for row in range(rows)]) for step in (3, 2, 1)
    )
    return [two, three, value, one]


def f32(*shape):
    return jax.ShapeDtypeStruct(shape, jnp.float32)


def cost(flops, moved):
    return pl.CostEstimate(flops=flops, bytes_accessed=moved, transcendentals=0)


def tables(side):
    half = side // 2
    index = np.arange(half)
    angle = 2.0 * math.pi / half * (np.outer(index, index) % half)
    cos = np.cos(angle) / math.sqrt(side)
    sin = -np.sin(angle) / math.sqrt(side)
    matrix = np.block([[cos, sin], [-sin, cos]])
    high = matrix.astype(BF16)
    low = (matrix - high.astype(np.float64)).astype(BF16)
    turn = -2.0 * math.pi / side * index
    twiddle = np.stack([np.cos(turn), np.sin(turn)]).astype(np.float32)
    lanes = np.ascontiguousarray(np.broadcast_to(twiddle[:, None, :], (2, 8, half)))
    rows = np.ascontiguousarray(np.broadcast_to(twiddle[:, :, None], (2, half, half)))
    return (
        np.concatenate([high, high, low], 0),
        np.concatenate([high.T, high.T, low.T], 1),
        np.concatenate([high.T, high.T, low.T], 0),
        np.concatenate([high, high, low], 1),
        lanes,
        rows,
    )


def dot(left, right):
    return jnp.dot(left, right, preferred_element_type=jnp.float32)


def halves(value):
    high = value.astype(BF16)
    low = (value - high.astype(jnp.float32)).astype(BF16)
    return high, low


def pack_extra(rows, extra, width):
    per = width // extra
    for group in range(rows // 8):
        yield group * 8, group // per * 8, group % per * extra


def pack_kernel(tile_ref, near_ref, far_ref, right_ref):
    side = tile_ref.shape[1]
    half = side // 2
    margin = far_ref.shape[1]
    extra = margin - half
    near_ref[:, 0:margin, :] = tile_ref[:, 0:margin, 0:half]
    far_ref[...] = tile_ref[:, 0:margin, half:]
    right_ref[:, 0:side, :] = tile_ref[:, :, 0:half]
    for row, packed, lane in pack_extra(side, extra, half):
        piece = tile_ref[:, row : row + 8, half:margin]
        right_ref[:, side + packed : side + packed + 8, lane : lane + extra] = piece
        if row < margin:
            near_ref[:, margin + packed : margin + packed + 8, lane : lane + extra] = piece


def peak_kernel(probe_ref, out_ref):
    re, im = probe_ref[0], probe_ref[1]
    top = jnp.max(re * re + im * im, axis=(0, 1), keepdims=True)
    out_ref[...] = jnp.broadcast_to(top, out_ref.shape)


def turned(load, steps, half, lanes):
    within = lax.rem(steps, half)
    first = lax.rem(lax.div(steps, half), 2)
    back = lax.rem(half - within, half)
    one = pltpu.roll(load(first), back, 1)
    two = pltpu.roll(load(1 - first), back, 1)
    stay = lanes < half - within
    return jnp.where(stay, one, two), jnp.where(stay, two, one)


def prepare_kernel(pos_ref, probe_ref, meas_ref, prot_ref, sorted_ref, twice):
    frames, side = meas_ref.shape[0], meas_ref.shape[1]
    half = side // 2
    for part in range(2):
        for tile in range(2):
            piece = probe_ref[part, :, tile * half : (tile + 1) * half]
            twice[part, tile, 0:side] = piece
            twice[part, tile, side : 2 * side] = piece
    step = 64
    lanes = lax.broadcasted_iota(jnp.int32, (step, half), 1)
    rows = lax.broadcasted_iota(jnp.int32, (side, side), 0)
    cols = lax.broadcasted_iota(jnp.int32, (side, side), 1)
    sort = jnp.where(rows == jnp.where(cols < half, 2 * cols, 2 * cols - side + 1), 1.0, 0.0).astype(BF16)
    unsort = jnp.where(cols == jnp.where(rows < half, 2 * rows, 2 * rows - side + 1), 1.0, 0.0).astype(BF16)

    @pl.loop(0, frames)
    def _(frame):
        dy = pos_ref[0, frame]
        dx = pos_ref[1, frame]
        for part in range(2):
            for row in range(0, side, step):
                one, two = turned(
                    lambda tile: twice[part, tile, pl.ds(side - dy + row, step), :], side - dx, half, lanes
                )
                prot_ref[frame, part, row : row + step, 0:half] = one
                prot_ref[frame, part, row : row + step, half:side] = two
        value = meas_ref[frame]
        total = None
        for _ in range(3):
            piece = value.astype(BF16)
            value = value - piece.astype(jnp.float32)
            term = dot(dot(unsort, piece).astype(BF16), sort)
            total = term if total is None else total + term
        sorted_ref[frame] = total


def frame_kernel(
    pos_ref, tile_ref, right_ref, near_ref, far_ref, corner_ref, prot_ref, meas_ref,
    fwd_right, fwd_left, inv_right, inv_left, lane_ref, row_ref,
    gt_ref, gr_ref, gz_ref, gc_ref, qs_ref,
    right_extra, corner_extra, obj_ref, left_in, right_in, mid, twice,
):
    frames, side = meas_ref.shape[0], meas_ref.shape[1]
    half = side // 2
    margin = far_ref.shape[1]
    extra = margin - half
    for row, packed, lane in pack_extra(side, extra, half):
        right_extra[:, row : row + 8, 0:extra] = right_ref[:, side + packed : side + packed + 8, lane : lane + extra]
        if row < margin:
            corner_extra[:, row : row + 8, 0:extra] = corner_ref[
                :, margin + packed : margin + packed + 8, lane : lane + extra
            ]
    lane_cos, lane_sin = lane_ref[0, 0:1], lane_ref[1, 0:1]

    def store_left(where, rows, tile, value):
        high, low = halves(value)
        lane = tile * half
        left_in[where, rows, lane : lane + half] = high
        left_in[where, rows, side + lane : side + lane + half] = low
        left_in[where, rows, 2 * side + lane : 2 * side + lane + half] = high

    def store_right(where, row, count, columns, value):
        high, low = halves(value)
        right_in[where, row : row + count, columns] = high
        right_in[where, side + row : side + row + count, columns] = low
        right_in[where, 2 * side + row : 2 * side + row + count, columns] = high

    step = 32
    lanes = lax.broadcasted_iota(jnp.int32, (step, half), 1)
    row_in = lax.broadcasted_iota(jnp.int32, (step, half), 0)
    for frame in range(frames):
        dy = pos_ref[0, frame]
        dx = pos_ref[1, frame]
        own_col = (lanes >= dx, lanes + half >= dx)
        for row in range(0, side, step):
            rows = slice(row, row + step)
            own_row = row_in + row >= dy
            wave = []
            for tile in range(2):
                columns = slice(tile * half, (tile + 1) * half)
                obj = []
                for part in range(2):
                    right = right_extra[part, rows] if tile else right_ref[part, rows]
                    value = jnp.where(own_col[tile], tile_ref[part, rows, columns], right)
                    if row < margin:
                        below = far_ref[part, rows] if tile else near_ref[part, rows]
                        corner = corner_extra[part, rows] if tile else corner_ref[part, rows]
                        value = jnp.where(own_row, value, jnp.where(own_col[tile], below, corner))
                    obj_ref[frame, part, rows, columns] = value
                    obj.append(value)
                pro_re = prot_ref[frame, 0, rows, columns]
                pro_im = prot_ref[frame, 1, rows, columns]
                wave.append((pro_re * obj[0] - pro_im * obj[1], pro_re * obj[1] + pro_im * obj[0]))
            (re0, im0), (re1, im1) = wave
            store_left(2 * frame, rows, 0, re0 + re1)
            store_left(2 * frame, rows, 1, im0 + im1)
            re, im = re0 - re1, im0 - im1
            store_left(2 * frame + 1, rows, 0, re * lane_cos - im * lane_sin)
            store_left(2 * frame + 1, rows, 1, re * lane_sin + im * lane_cos)
        for which in range(2):
            mid[2 * frame + which] = dot(left_in[2 * frame + which], fwd_right[...])

    for frame in range(frames):
        for row in range(0, half, step):
            top, low = slice(row, row + step), slice(half + row, half + row + step)
            row_cos, row_sin = row_ref[0, top], row_ref[1, top]
            for which in range(2):
                columns = slice(which * half, (which + 1) * half)
                top_re, top_im = mid[2 * frame + which, top, 0:half], mid[2 * frame + which, top, half:side]
                low_re, low_im = mid[2 * frame + which, low, 0:half], mid[2 * frame + which, low, half:side]
                store_right(2 * frame, row, step, columns, top_re + low_re)
                store_right(2 * frame, half + row, step, columns, top_im + low_im)
                re, im = top_re - low_re, top_im - low_im
                store_right(2 * frame + 1, row, step, columns, re * row_cos - im * row_sin)
                store_right(2 * frame + 1, half + row, step, columns, re * row_sin + im * row_cos)
        for which in range(2):
            mid[2 * frame + which] = dot(fwd_left[...], right_in[2 * frame + which])

    for frame in range(frames):
        for which in range(2):
            for row in range(0, half, step):
                re = mid[2 * frame + which, row : row + step]
                im = mid[2 * frame + which, half + row : half + row + step]
                ampl = meas_ref[frame, which * half + row : which * half + row + step]
                factor = ampl * lax.rsqrt(jnp.maximum(re * re + im * im, 0.25)) - 1.0
                store_right(2 * frame + which, row, step, slice(0, side), factor * re)
                store_right(2 * frame + which, half + row, step, slice(0, side), factor * im)
            mid[2 * frame + which] = dot(inv_left[...], right_in[2 * frame + which])

    for frame in range(frames):
        for row in range(0, half, step):
            top, low = slice(row, row + step), slice(half + row, half + row + step)
            row_cos, row_sin = row_ref[0, top], row_ref[1, top]
            for which in range(2):
                columns = slice(which * half, (which + 1) * half)
                even_re, even_im = mid[2 * frame, top, columns], mid[2 * frame, low, columns]
                odd_re, odd_im = mid[2 * frame + 1, top, columns], mid[2 * frame + 1, low, columns]
                re = odd_re * row_cos + odd_im * row_sin
                im = odd_im * row_cos - odd_re * row_sin
                store_left(2 * frame + which, top, 0, even_re + re)
                store_left(2 * frame + which, top, 1, even_im + im)
                store_left(2 * frame + which, low, 0, even_re - re)
                store_left(2 * frame + which, low, 1, even_im - im)
        for which in range(2):
            mid[2 * frame + which] = dot(left_in[2 * frame + which], inv_right[...])

    step = 8
    lanes = lax.broadcasted_iota(jnp.int32, (step, half), 1)
    row_in = lax.broadcasted_iota(jnp.int32, (step, half), 0)
    places = {row: (packed, lane) for row, packed, lane in pack_extra(side, extra, half)}
    for row in range(0, side, step):
        rows = slice(row, row + step)
        total = {}
        for frame in range(frames):
            dy = pos_ref[0, frame]
            dx = pos_ref[1, frame]
            masks = []
            for tile in range(2):
                own_col = lanes + tile * half >= dx
                far_col = jnp.logical_not(own_col)
                if row < margin:
                    own_row = row_in + row >= dy
                    far_row = jnp.logical_not(own_row)
                    masks.append(
                        {"t": own_row & own_col, "r": own_row & far_col, "b": far_row & own_col, "c": far_row & far_col}
                    )
                else:
                    masks.append({"t": own_col, "r": far_col})
            even_re, even_im = mid[2 * frame, rows, 0:half], mid[2 * frame, rows, half:side]
            odd_re, odd_im = mid[2 * frame + 1, rows, 0:half], mid[2 * frame + 1, rows, half:side]
            re = odd_re * lane_cos + odd_im * lane_sin
            im = odd_im * lane_cos - odd_re * lane_sin
            for tile in range(2):
                columns = slice(tile * half, (tile + 1) * half)
                chi_re = even_re - re if tile else even_re + re
                chi_im = even_im - im if tile else even_im + im
                pro_re = prot_ref[frame, 0, rows, columns]
                pro_im = prot_ref[frame, 1, rows, columns]
                obj_re = obj_ref[frame, 0, rows, columns]
                obj_im = obj_ref[frame, 1, rows, columns]
                for part, value in enumerate(
                    (pro_re * chi_re + pro_im * chi_im, pro_re * chi_im - pro_im * chi_re)
                ):
                    for name, mask in masks[tile].items():
                        piece = jnp.where(mask, value, 0.0)
                        key = (name, part, tile)
                        total[key] = piece if frame == 0 else total[key] + piece
                for index, value in enumerate(
                    (
                        obj_re * chi_re + obj_im * chi_im,
                        obj_re * chi_im - obj_im * chi_re,
                        obj_re * obj_re + obj_im * obj_im,
                    )
                ):
                    twice[frame, index, tile, row : row + step] = value
                    if row < margin:
                        twice[frame, index, tile, side + row : side + row + step] = value
        packed, lane = places[row]
        for part in range(2):
            gt_ref[part, rows, 0:half] = total["t", part, 0]
            gt_ref[part, rows, half:side] = total["t", part, 1]
            gr_ref[part, rows] = total["r", part, 0]
            gr_ref[part, side + packed : side + packed + 8, lane : lane + extra] = total["r", part, 1][:, 0:extra]
            if row < margin:
                gz_ref[part, rows] = total["b", part, 0]
                gz_ref[part, margin + row : margin + row + step] = total["b", part, 1]
                gc_ref[part, rows] = total["c", part, 0]
                base = margin + packed
                gc_ref[part, base : base + 8, lane : lane + extra] = total["c", part, 1][:, 0:extra]

    depth = qs_ref.shape[2]
    step = min(32, depth)
    lanes = lax.broadcasted_iota(jnp.int32, (step, half), 1)
    for row in range(0, side, step):
        for index in range(3):
            sums = None
            for frame in range(frames):
                dy = pos_ref[0, frame]
                dx = pos_ref[1, frame]
                pair = turned(
                    lambda tile: twice[frame, index, tile, pl.ds(dy + row, step), :], dx, half, lanes
                )
                sums = pair if sums is None else (sums[0] + pair[0], sums[1] + pair[1])
            place = slice(row % depth, row % depth + step)
            qs_ref[row // depth, index, place, 0:half] = sums[0]
            qs_ref[row // depth, index, place, half:side] = sums[1]


def update_kernel(old_ref, *refs):
    terms, out_ref = refs[:-1], refs[-1]

    def total(index):
        values = [term[index] for term in terms]
        while len(values) > 1:
            values = [values[at] + values[at + 1] for at in range(0, len(values), 2)]
        return values[0]

    weight = total(2) + 1.0
    for part in range(2):
        value = old_ref[part] + total(part) / weight
        for copy in range(out_ref.shape[0]):
            out_ref[copy, part] = value


def finish_kernel(peak_ref, tile_ref, grad_ref, right_ref, down_ref, corner_ref, new_ref, out_ref, probe_ref):
    side = tile_ref.shape[1]
    half = side // 2
    margin = down_ref.shape[1] // 2
    extra = margin - half
    depth = new_ref.shape[2]
    for block in range(new_ref.shape[0]):
        probe_ref[:, block * depth : (block + 1) * depth, :] = new_ref[block]
    largest = peak_ref[...]
    step = 8
    for row, packed, lane in pack_extra(side, extra, half):
        place = slice(row, row + step)
        for part in range(2):
            one = grad_ref[part, place, 0:half] + right_ref[part, place]
            two = grad_ref[part, place, half:side]
            piece = right_ref[part, side + packed : side + packed + 8, lane : lane + extra]
            if row < margin:
                one = one + down_ref[part, place] + corner_ref[part, place]
                two = two + down_ref[part, margin + row : margin + row + step]
                piece = piece + corner_ref[part, margin + packed : margin + packed + 8, lane : lane + extra]
            out_ref[part, place, 0:half] = tile_ref[part, place, 0:half] + one / largest
            out_ref[part, place, half:side] = tile_ref[part, place, half:side] + two / largest
            out_ref[part, place, half:margin] += piece / largest[:, 0:extra]


def body(object_field, probe_field, measured, positions):
    side = probe_field.shape[1]
    half = side // 2
    margin = HALO
    extra = margin - half
    frames = measured.shape[0]
    n_row, n_col = lax.axis_size("row"), lax.axis_size("col")
    fwd_right, fwd_left, inv_right, inv_left, lane_tw, row_tw = tables(side)
    wide = side + side * extra // half
    tall = margin + margin * extra // half

    near, far, right = pl.pallas_call(
        pack_kernel,
        out_shape=(f32(2, tall, half), f32(2, margin, half), f32(2, wide, half)),
        in_specs=[VMEM],
        out_specs=(VMEM,) * 3,
        cost_estimate=cost(10**6, 2 * 10**6),
        compiler_params=PARAMS,
    )(object_field)
    near = shifted(near, "row", -1)
    far = shifted(far, "row", -1)
    right = shifted(right, "col", -1)
    near, probe, ampl = lax.optimization_barrier((near, probe_field, measured))
    peak = pl.pallas_call(
        peak_kernel,
        out_shape=f32(8, half),
        in_specs=[VMEM],
        out_specs=VMEM,
        cost_estimate=cost(10**6, 2 * 10**6),
        compiler_params=PARAMS,
    )(probe)
    corner = shifted(near, "col", -1)
    places = positions.T
    prot, ampl = pl.pallas_call(
        prepare_kernel,
        out_shape=(f32(frames, 2, side, side), f32(frames, side, side)),
        in_specs=[SMEM, VMEM, VMEM],
        out_specs=(VMEM, VMEM),
        scratch_shapes=[pltpu.VMEM((2, 2, 2 * side, half), jnp.float32)],
        cost_estimate=cost(3 * 10**9, 6 * 10**6),
        compiler_params=PARAMS,
    )(places, probe, ampl)
    prot, peak = lax.optimization_barrier((prot, peak))
    depth = side // n_col
    g_tile, g_right, g_down, g_corner, sums = pl.pallas_call(
        frame_kernel,
        out_shape=(
            f32(2, side, side),
            f32(2, wide, half),
            f32(2, 2 * margin, half),
            f32(2, tall, half),
            f32(n_col, 3, depth, side),
        ),
        in_specs=[SMEM] + [VMEM] * 13,
        out_specs=(VMEM,) * 5,
        scratch_shapes=[
            pltpu.VMEM((2, side, half), jnp.float32),
            pltpu.VMEM((2, margin, half), jnp.float32),
            pltpu.VMEM((frames, 2, side, side), jnp.float32),
            pltpu.VMEM((2 * frames, side, 3 * side), BF16),
            pltpu.VMEM((2 * frames, 3 * side, side), BF16),
            pltpu.VMEM((2 * frames, side, side), jnp.float32),
            pltpu.VMEM((frames, 3, 2, side + margin, half), jnp.float32),
        ],
        cost_estimate=cost(6 * 10**9, 12 * 10**6),
        compiler_params=PARAMS,
    )(
        places, object_field, right, near, far, corner, prot, ampl,
        fwd_right, fwd_left, inv_right, inv_left, lane_tw, row_tw,
    )

    from_above = shifted(g_down, "row", 1)
    part = jnp.sum(lax.all_to_all(sums, "col", 0, 0), 0)
    part, from_above, g_right = lax.optimization_barrier((part, from_above, g_right))
    old = lax.dynamic_slice_in_dim(probe_field, lax.axis_index("col") * depth, depth, 1)
    terms = row_terms(part)
    from_left = shifted(g_right, "col", 1)
    g_corner, terms[0] = lax.optimization_barrier((g_corner, terms[0]))
    from_corner = diagonal(g_corner)
    new = pl.pallas_call(
        update_kernel,
        out_shape=f32(n_col, 2, depth, side),
        in_specs=[VMEM] * (1 + len(terms)),
        out_specs=VMEM,
        cost_estimate=cost(10**10, 10**6),
        compiler_params=PARAMS,
    )(old, *terms)
    new, from_left = lax.optimization_barrier((new, from_left))
    new = lax.all_to_all(new, "col", 0, 0)
    new_object, new_probe = pl.pallas_call(
        finish_kernel,
        out_shape=(f32(2, side, side), f32(2, side, side)),
        in_specs=[VMEM] * 7,
        out_specs=(VMEM, VMEM),
        cost_estimate=cost(10**6, 4 * 10**6),
        compiler_params=PARAMS,
    )(peak, object_field, g_tile, from_left, from_above, from_corner, new)
    return (new_object, new_probe)


def solution(mesh):
    in_specs = (P(None, "row", "col"), P(), P("row", "col", None), P("row", "col"))
    out_specs = (P(None, "row", "col"), P())
    return jax.shard_map(body, mesh=mesh, in_specs=in_specs, out_specs=out_specs, check_vma=False)
```
